256 devices in a mesh: section: 16 (over z_lo, x, core), tensor: 4 (over z_hi), dp: 4 (over y).
Axes of the slice: x: 4, y: 4, z: 8 (z_hi: 4, z_lo: 2; z = z_hi * 2 + z_lo), core: 2. Of those that a mesh axis runs over, the one named last changes fastest.
Arguments:
- attn_a: bfloat16 [16, 512, 7168], P('section', 'dp', 'tensor'), may hold values from -15 to 15, as said below
- attn_b: bfloat16 [16, 512, 7168], P('section', 'dp', 'tensor'), may hold values from -15 to 15, as said below
- w_down: bfloat16 [16, 7168, 768], P('section', 'tensor'), may hold values from -0.0625 to 0.0625
- q_gain: bfloat16 [16, 768], P('section'), may hold values from 0.099609375 to 1.8984375
- w_up: bfloat16 [16, 768, 12288], P('section', None, 'tensor'), may hold values from -0.21875 to 0.21875
- dq_a: bfloat16 [16, 512, 12288], P('section', 'dp', 'tensor'), may hold values from -6 to 6
- dq_b: bfloat16 [16, 512, 12288], P('section', 'dp', 'tensor'), may hold values from -6 to 6
Outputs:
- grad_down: bfloat16 [16, 7168, 768], P('section', ('tensor', 'dp'))
- grad_gain: bfloat16 [16, 768], P('section', 'dp')
- grad_up: bfloat16 [16, 768, 12288], P('section', 'dp', 'tensor')
The draws below stay inside these ranges and needn't reach their ends.
Inputs may be any that keep to these rules, and one draw needn't show every extreme that they name: attn_a is real-valued. attn_b is real-valued.
All inputs are finite; a program needn't handle non-finite values.
Results may differ from the reference program's by a relative error of at most 0.035.
Values may be sent and summed in bfloat16 or wider, within the bound.
A program may use at most 128 MiB of HBM per device.

```python
import math
import jax
import jax.numpy as jnp
from jax import lax

D = 7168
QL = 768
HQ = 12288
TOK_DEV = 128
TOKENS = 512
N_SECTION = 16
N_DP = 4


def attn_draw(key):
    key_base, key_rows = jax.random.split(key, 2)
    base = jnp.clip(jax.random.normal(key_base, (N_SECTION, TOKENS, D), jnp.float32), -4.0, 4.0)
    row_scale = jnp.exp(jax.random.uniform(key_rows, (N_SECTION, TOKENS, 1), jnp.float32, 0.0, math.log(10.0)))
    return (base * row_scale / 3.0).astype(jnp.bfloat16)


def draw_attn_a(key, part):
    key = jax.random.fold_in(key, 11)
    return attn_draw(key)


def draw_attn_b(key, part):
    key = jax.random.fold_in(key, 12)
    return attn_draw(key)


def shard_levels(rng, extent, shards, smallest, largest):
    level, own = 1.0, jax.random.fold_in(rng, 6)
    for position, parts in shards:
        steps = jnp.exp(jax.random.uniform(jax.random.fold_in(own, position), (parts,), jnp.float32, smallest / len(shards), largest / len(shards)))
        level = level * jnp.repeat(steps, extent[position] // parts).reshape([-1 if axis == position else 1 for axis in range(len(extent))])
    return level


def scatter_about(rng, dims, deviation, reach, cuts=(), held_as=jnp.bfloat16):
    gain = shard_levels(rng, dims, cuts, -0.22, 0.18) if cuts else 1.0
    entries = jax.random.normal(rng, dims, jnp.float32) * deviation * gain
    return jnp.minimum(jnp.maximum(entries, -reach), reach).astype(held_as)


def setup_inputs(seed: int = 0) -> dict:
    streams_of = jax.random.split(jax.random.key(seed), 8)
    attn_a = draw_attn_a(jax.random.fold_in(streams_of[7], 71), 0)
    attn_b = draw_attn_b(jax.random.fold_in(streams_of[7], 71), 0)
    w_down = scatter_about(streams_of[2], (N_SECTION, D, QL), D ** -0.5, 0.0625, ((0, 16), (1, 4)))
    q_gain = jnp.clip(1.0 + 0.18 * jax.random.normal(streams_of[3], (N_SECTION, QL), jnp.float32), 0.099609375, 1.8984375).astype(jnp.bfloat16)
    w_up = scatter_about(streams_of[4], (N_SECTION, QL, HQ), QL ** -0.5, 0.21875, ((0, 16), (2, 4)))
    dq_a = scatter_about(streams_of[5], (N_SECTION, TOKENS, HQ), 1.0, 6.0, ((0, 16), (1, 4), (2, 4)))
    dq_b = scatter_about(streams_of[6], (N_SECTION, TOKENS, HQ), 1.0, 6.0, ((0, 16), (1, 4), (2, 4)))
    return dict(attn_a=attn_a, attn_b=attn_b, w_down=w_down, q_gain=q_gain, w_up=w_up, dq_a=dq_a, dq_b=dq_b)


EPSILON = 1e-06

def section_norm(latent, gain_row):
    inverse = lax.rsqrt(lax.optimization_barrier(jnp.mean(latent * latent, axis=-1, keepdims=True)) + EPSILON)
    normed = (latent * inverse * gain_row).astype(jnp.bfloat16)
    return (normed, inverse)

def norm_back(grad_normed, latent, inverse, gain_row):
    scaled = grad_normed * gain_row
    grad_gain = lax.optimization_barrier(jnp.sum(grad_normed * latent * inverse, axis=0))
    grad_latent = inverse * scaled - latent * inverse ** 3 * lax.optimization_barrier(jnp.mean(scaled * latent, axis=-1, keepdims=True))
    return (grad_latent.astype(jnp.bfloat16), grad_gain)

def direction_terms(hidden, grad_query, down_weight, gain_row, up_weight):
    latent = jnp.dot(hidden, down_weight, preferred_element_type=jnp.float32)
    normed, inverse = section_norm(latent, gain_row)
    grad_up = jnp.dot(normed.T, grad_query, preferred_element_type=jnp.float32)
    grad_normed = jnp.dot(grad_query, up_weight.T, preferred_element_type=jnp.float32)
    grad_latent, grad_gain = norm_back(grad_normed, latent, inverse, gain_row)
    grad_down = jnp.dot(hidden.T, grad_latent, preferred_element_type=jnp.float32)
    return (grad_down, grad_gain, grad_up)

def reference(attn_a, attn_b, w_down, q_gain, w_up, dq_a, dq_b):
    rising = jnp.cumsum(attn_a.astype(jnp.float32), axis=0).astype(jnp.bfloat16)
    falling = jnp.flip(jnp.cumsum(jnp.flip(attn_b.astype(jnp.float32), 0), axis=0), 0).astype(jnp.bfloat16)

    def by_block(array):
        return array.reshape(N_DP, TOK_DEV, array.shape[-1])

    def one_section(section_args):
        rise_s, fall_s, grad_a, grad_b, down_weight, gain_weight, up_weight = section_args
        gain_row = gain_weight.astype(jnp.float32)

        def one_block(block_args):
            rise_blk, fall_blk, grad_blk_a, grad_blk_b = block_args
            down_a, gain_a, up_a = direction_terms(rise_blk, grad_blk_a, down_weight, gain_row, up_weight)
            down_b, gain_b, up_b = direction_terms(fall_blk, grad_blk_b, down_weight, gain_row, up_weight)
            return ((down_a + down_b).astype(jnp.bfloat16), (gain_a + gain_b).astype(jnp.bfloat16), (up_a + up_b).astype(jnp.bfloat16))
        down_parts, gain_parts, up_parts = lax.map(one_block, (by_block(rise_s), by_block(fall_s), by_block(grad_a), by_block(grad_b)))
        return (lax.optimization_barrier(jnp.sum(down_parts.astype(jnp.float32), axis=0)).astype(jnp.bfloat16), lax.optimization_barrier(jnp.sum(gain_parts.astype(jnp.float32), axis=0)).astype(jnp.bfloat16), lax.optimization_barrier(jnp.sum(up_parts.astype(jnp.float32), axis=0)).astype(jnp.bfloat16))
    down_sum, gain_sum, up_sum = lax.map(one_section, (rising, falling, dq_a, dq_b, w_down, q_gain, w_up))

    def mirrored(piece):
        return (piece.astype(jnp.float32) + jnp.flip(piece, 0).astype(jnp.float32)).astype(jnp.bfloat16)
    return (mirrored(down_sum), mirrored(gain_sum), mirrored(up_sum))
```

```python
import functools

import jax
import jax.numpy as jnp
from jax import lax
from jax.experimental import pallas as pl
from jax.experimental.pallas import tpu as pltpu
from jax.sharding import PartitionSpec as P

EPSILON = 1e-06
MESH = pl.DeviceIdType.MESH
F32 = jnp.float32
BF16 = jnp.bfloat16

TOK = 128
DM = 1792
QL = 768
HQ = 3072
CH = 8
BLK = TOK // CH
SUB = TOK // 4
DSH = DM // 4
USH = QL // 4
UCH = 4
UW = HQ // UCH
DCH = 2
DW = QL // DCH


def rows(i, n):
    return pl.ds(pl.multiple_of(i * n, n), n)


def kernel(
    attn_a, attn_b, w_down, gain, w_up, dq_a, dq_b,
    out_down, out_gain, out_up,
    att, xin, tot, got, pout, pfx, hid, dq, wd, wu,
    gnp, gnr, latp, latr, nz, gz, ntl, nall, gl, htl, hall,
    ubuf, urec, dbuf, drec, gbuf, grec,
    lsem, ss, rs,
):
    s, t, d = lax.axis_index("section"), lax.axis_index("tensor"), lax.axis_index("dp")
    chip, core = s // 2, s % 2

    def at_chip(j):
        return (j * 2 + core, t, d)

    def at_tensor(j):
        return (s, j, d)

    def at_dp(j):
        return (s, t, j)

    other_core = (chip * 2 + 1 - core, t, d)
    mirror = (15 - s, t, d)
    chips = [((chip + k) % CH) for k in range(1, CH)]
    tens = [((t + k) % 4) for k in range(1, 4)]
    dps = [((d + k) % 4) for k in range(1, 4)]

    counter = [0]
    sent = []

    def send(src, dst, to):
        i = counter[0]
        counter[0] += 1
        copy = pltpu.make_async_remote_copy(
            src_ref=src, dst_ref=dst, send_sem=ss.at[i], recv_sem=rs.at[i],
            device_id=to, device_id_type=MESH,
        )
        copy.start()
        sent.append(copy)
        return copy

    loads = []
    for i, (src, dst) in enumerate((
        (attn_a, att.at[0]),
        (attn_b, att.at[1]),
        (dq_a, dq.at[d, pl.ds(0, TOK)]),
        (dq_b, dq.at[d, pl.ds(TOK, TOK)]),
        (w_up, wu),
        (w_down, wd),
    )):
        c = pltpu.make_async_copy(src, dst, lsem.at[i])
        c.start()
        loads.append(c)

    barrier = pltpu.get_barrier_semaphore()
    partners = (
        [other_core, mirror]
        + [at_chip(j) for j in chips]
        + [at_tensor(j) for j in tens]
        + [at_dp(j) for j in dps]
    )
    for p in partners:
        pl.semaphore_signal(barrier, inc=1, device_id=p, device_id_type=MESH)
    pl.semaphore_wait(barrier, len(partners))

    loads[0].wait()
    loads[1].wait()
    swap = send(att.at[1 - core], xin, other_core)

    up, dn = (d + 1) % 4, (d + 3) % 4
    dq_up_a = send(dq_a, dq.at[d, pl.ds(0, TOK)], at_dp(up))
    dq_dn_b = send(dq_b, dq.at[d, pl.ds(TOK, TOK)], at_dp(dn))
    dq_up_b = send(dq_b, dq.at[d, pl.ds(TOK, TOK)], at_dp(up))
    dq_dn_a = send(dq_a, dq.at[d, pl.ds(0, TOK)], at_dp(dn))

    swap.wait_recv()
    tot[...] = (att[core].astype(F32) + xin[...].astype(F32)).astype(BF16)
    ph1 = [send(tot.at[rows(j, BLK)], got.at[chip], at_chip(j)) for j in chips]
    got[chip] = tot[rows(chip, BLK)]

    loads[2].wait()
    loads[3].wait()
    loads[4].wait()
    for m in range(2):
        gnp[m] = lax.dot_general(
            dq[d, m * TOK:(m + 1) * TOK], wu[...], (((1,), (1,)), ((), ())),
            preferred_element_type=F32,
        ).astype(BF16)
    gn = [send(gnp.at[:, rows(j, SUB)], gnr.at[k], at_tensor(j)) for k, j in enumerate(tens)]

    for c in ph1:
        c.wait_recv()
    run = jnp.zeros((BLK, DM), F32)
    for i in range(CH):
        j = i + core * (CH - 1 - 2 * i)
        pout[j] = run.astype(BF16)
        if i < CH - 1:
            run = run + got[j].astype(F32)
    ph2 = [send(pout.at[j], pfx.at[rows(chip, BLK)], at_chip(j)) for j in chips]
    pfx[rows(chip, BLK)] = pout[chip]
    for c in ph2:
        c.wait_recv()
    mine = pfx[...].astype(F32) + att[core].astype(F32)
    tot2 = xin
    tot2[...] = (mine + xin[...].astype(F32)).astype(BF16)
    back = send(tot2, hid.at[core], other_core)
    hid[core] = mine.astype(BF16)
    loads[5].wait()
    back.wait_recv()
    for m in range(2):
        latp[m] = jnp.dot(hid[m], wd[...], preferred_element_type=F32).astype(BF16)
    lt = [send(latp.at[:, rows(j, SUB)], latr.at[k], at_tensor(j)) for k, j in enumerate(tens)]

    for m in range(2):
        for q in range(4):
            for e in range(0, DSH, 64):
                lo = q * DSH + e
                base = lo // 128 * 128
                if lo % 128 == 0 and e + 128 <= DSH:
                    htl[q, e:e + 128, m * TOK:(m + 1) * TOK] = hid[m, :, lo:lo + 128].T
                elif lo % 128 == 0:
                    htl[q, e:e + 64, m * TOK:(m + 1) * TOK] = hid[m, :, base:base + 128].T[0:64]
                elif e == 0:
                    htl[q, 0:64, m * TOK:(m + 1) * TOK] = hid[m, :, base:base + 128].T[64:128]
    ht = [send(htl.at[j], hall.at[d], at_dp(j)) for j in dps]
    hall[d] = htl[d]

    for c in gn + lt:
        c.wait_recv()

    def total(part, recv):
        x = part[:, rows(t, SUB)].astype(F32)
        for k in range(3):
            x = x + recv[k].astype(F32)
        return x.reshape(2 * SUB, QL)

    lat = total(latp, latr)
    gnrm = total(gnp, gnr)
    g = gain[...].astype(F32)
    inv = lax.rsqrt(jnp.mean(lat * lat, axis=-1, keepdims=True) + EPSILON)
    nz[t] = (lat * inv * g).astype(BF16)
    an = [send(nz.at[t], nz.at[t], at_tensor(j)) for j in tens]
    scaled = gnrm * g
    glat = inv * scaled - lat * (inv * inv * inv) * jnp.mean(scaled * lat, axis=-1, keepdims=True)

    def hi_lo(v):
        hi = v.astype(BF16)
        lo = (v - hi.astype(F32)).astype(BF16)
        r = lax.broadcasted_iota(jnp.int32, (16, QL), 0)
        return jnp.where(r == 0, hi.astype(F32), jnp.where(r == 1, lo.astype(F32), 0.0)).astype(BF16)

    gz[t, 0:2 * SUB] = glat.astype(BF16)
    gz[t, 2 * SUB:2 * SUB + 16] = hi_lo(jnp.sum(gnrm * lat * inv, axis=0, keepdims=True))
    ag = [send(gz.at[t], gz.at[t], at_tensor(j)) for j in tens]

    dq_up_a.wait_recv()
    fw_up = send(dq.at[dn, pl.ds(0, TOK)], dq.at[dn, pl.ds(0, TOK)], at_dp(up))
    dq_dn_b.wait_recv()
    fw_dn = send(dq.at[up, pl.ds(TOK, TOK)], dq.at[up, pl.ds(TOK, TOK)], at_dp(dn))

    for c in an:
        c.wait_recv()
    for m in range(2):
        full = jnp.concatenate([nz[k, m * SUB:(m + 1) * SUB] for k in range(4)], axis=0)
        for q in range(QL // 64):
            if q % 2 == 0:
                tr = full[:, q * 64:q * 64 + 128].T
            dst, off = q * 64 // USH, q * 64 % USH
            ntl[dst, off:off + 64, m * TOK:(m + 1) * TOK] = tr[(q % 2) * 64:(q % 2) * 64 + 64]
    nt = [send(ntl.at[j], nall.at[d], at_dp(j)) for j in dps]
    nall[d] = ntl[d]

    for c in ag:
        c.wait_recv()
    for m in range(2):
        for k in range(4):
            gl[d, m * TOK + k * SUB:m * TOK + (k + 1) * SUB] = gz[k, m * SUB:(m + 1) * SUB]

    def gain_rows(parts):
        v = jnp.zeros((1, QL), F32)
        for x in parts:
            v = v + jnp.sum(x.astype(F32), axis=0, keepdims=True)
        return v

    gl[d, 2 * TOK:2 * TOK + 16] = hi_lo(gain_rows([gz[k, 2 * SUB:2 * SUB + 16] for k in range(4)]))
    ga = [send(gl.at[d], gl.at[d], at_dp(j)) for j in dps]

    for c in nt:
        c.wait_recv()
    for c in (dq_up_b, dq_dn_a, fw_up, fw_dn):
        c.wait_recv()
    ups = []
    for n in range(UCH):
        acc = jnp.zeros((USH, UW), F32)
        for k in range(4):
            acc = acc + jnp.dot(
                nall[k], dq[k, :, n * UW:(n + 1) * UW], preferred_element_type=F32
            )
        ubuf[n] = acc.astype(BF16)
        ups.append(send(ubuf.at[n], urec.at[n], mirror))

    for c in ga + ht:
        c.wait_recv()
    gbuf[...] = jnp.broadcast_to(
        gain_rows([gl[k, 2 * TOK:2 * TOK + 16] for k in range(4)]), (16, QL)
    ).astype(BF16)
    gsend = send(gbuf, grec, mirror)
    downs = []
    for n in range(DCH):
        acc = jnp.zeros((DSH, DW), F32)
        for k in range(4):
            acc = acc + jnp.dot(
                hall[k], gl[k, 0:2 * TOK, n * DW:(n + 1) * DW], preferred_element_type=F32
            )
        dbuf[n] = acc.astype(BF16)
        downs.append(send(dbuf.at[n], drec.at[n], mirror))

    gsend.wait_recv()
    both = (gbuf[0:1].astype(F32) + grec[0:1].astype(F32))
    pick = both[:, 0:USH]
    for q in range(1, 4):
        pick = jnp.where(d == q, both[:, q * USH:(q + 1) * USH], pick)
    out_gain[...] = pick.astype(BF16)
    for n in range(UCH):
        ups[n].wait_recv()
        out_up[:, n * UW:(n + 1) * UW] = (ubuf[n].astype(F32) + urec[n].astype(F32)).astype(BF16)
    for n in range(DCH):
        downs[n].wait_recv()
        out_down[:, n * DW:(n + 1) * DW] = (dbuf[n].astype(F32) + drec[n].astype(F32)).astype(BF16)
    for c in sent:
        c.wait_send()


NCOPY = 1 + 4 + 7 + 3 + 7 + 1 + 3 + 3 + 3 + 3 + 2 + 3 + 3 + UCH + 1 + DCH


def local(attn_a, attn_b, w_down, q_gain, w_up, dq_a, dq_b):
    anywhere = pl.BlockSpec(memory_space=pl.ANY)
    vmem = pl.BlockSpec(memory_space=pltpu.VMEM)
    shapes = [
        (2, TOK, DM), (TOK, DM), (TOK, DM), (CH, BLK, DM), (CH, BLK, DM), (TOK, DM), (2, TOK, DM),
        (4, 2 * TOK, HQ), (DM, QL), (QL, HQ),
        (2, TOK, QL), (3, 2, SUB, QL), (2, TOK, QL), (3, 2, SUB, QL),
        (4, 2 * SUB, QL), (4, 2 * SUB + 16, QL),
        (4, USH, 2 * TOK), (4, USH, 2 * TOK), (4, 2 * TOK + 16, QL),
        (4, DSH, 2 * TOK), (4, DSH, 2 * TOK),
        (UCH, USH, UW), (UCH, USH, UW), (DCH, DSH, DW), (DCH, DSH, DW), (16, QL), (16, QL),
    ]
    down, gain, up = pl.pallas_call(
        kernel,
        out_shape=(
            jax.ShapeDtypeStruct((DSH, QL), BF16),
            jax.ShapeDtypeStruct((1, USH), BF16),
            jax.ShapeDtypeStruct((USH, HQ), BF16),
        ),
        in_specs=[anywhere, anywhere, anywhere, vmem, anywhere, anywhere, anywhere],
        out_specs=(vmem, vmem, vmem),
        scratch_shapes=[pltpu.VMEM(x, BF16) for x in shapes] + [
            pltpu.SemaphoreType.DMA((6,)),
            pltpu.SemaphoreType.DMA((NCOPY,)),
            pltpu.SemaphoreType.DMA((NCOPY,)),
        ],
        compiler_params=pltpu.CompilerParams(
            collective_id=0, has_side_effects=True, vmem_limit_bytes=56 * 2**20
        ),
        name="sections",
    )(attn_a[0], attn_b[0], w_down[0], q_gain, w_up[0], dq_a[0], dq_b[0])
    return down[None], gain, up[None]


def solution(mesh):
    return jax.shard_map(
        local,
        mesh=mesh,
        in_specs=(
            P("section", "dp", "tensor"),
            P("section", "dp", "tensor"),
            P("section", "tensor", None),
            P("section", None),
            P("section", None, "tensor"),
            P("section", "dp", "tensor"),
            P("section", "dp", "tensor"),
        ),
        out_specs=(
            P("section", ("tensor", "dp"), None),
            P("section", "dp"),
            P("section", "dp", "tensor"),
        ),
        check_vma=False,
    )
```

```python
import functools

import jax
import jax.numpy as jnp
from jax import lax
from jax.experimental import pallas as pl
from jax.experimental.pallas import tpu as pltpu
from jax.sharding import PartitionSpec as P

EPSILON = 1e-06
MESH = pl.DeviceIdType.MESH
F32 = jnp.float32
BF16 = jnp.bfloat16

TOK = 128
DM = 1792
QL = 768
HQ = 3072
CH = 8
BLK = TOK // CH
SUB = TOK // 4
DSH = DM // 4
USH = QL // 4
UCH = 4
UW = HQ // UCH
DCH = 2
DW = QL // DCH
HW = HQ // 2
NCOPY = 96


def rows(i, n):
    return pl.ds(pl.multiple_of(i * n, n), n)


def kernel(
    attn_a, attn_b, w_down, gain, w_up, dq_a, dq_b,
    u_own, u_rec, d_own, d_rec, g_own, g_rec,
    att, xin, tot, got, pout, pfx, hid, dq, wd, wu,
    gnp, gnr, latp, latr, nz, gz, ntl, nall, gl, gg, htl, hall,
    ubuf, dbuf, gbuf,
    lsem, ss, rs,
):
    s, t, d = lax.axis_index("section"), lax.axis_index("tensor"), lax.axis_index("dp")
    chip, core = s // 2, s % 2

    def at_chip(j):
        return (j * 2 + core, t, d)

    def at_tensor(j):
        return (s, j, d)

    def at_dp(j):
        return (s, t, j)

    other_core = (chip * 2 + 1 - core, t, d)
    mirror = (15 - s, t, d)
    chips = [((chip + k) % CH) for k in range(1, CH)]
    tens = [((t + k) % 4) for k in range(1, 4)]
    dps = [((d + k) % 4) for k in range(1, 4)]
    up, dn = (d + 1) % 4, (d + 3) % 4
    lo, hi = pl.ds(0, TOK), pl.ds(TOK, TOK)

    counter = [0]
    sent = []

    def send(src, dst, to):
        i = counter[0]
        counter[0] += 1
        copy = pltpu.make_async_remote_copy(
            src_ref=src, dst_ref=dst, send_sem=ss.at[i], recv_sem=rs.at[i],
            device_id=to, device_id_type=MESH,
        )
        copy.start()
        sent.append(copy)
        return copy

    loads = []

    def load(src, dst):
        c = pltpu.make_async_copy(src, dst, lsem.at[len(loads)])
        c.start()
        loads.append(c)
        return c

    ld_a = load(attn_a, att.at[0])
    ld_b = load(attn_b, att.at[1])

    barrier = pltpu.get_barrier_semaphore()
    partners = (
        [other_core, mirror]
        + [at_chip(j) for j in chips]
        + [at_tensor(j) for j in tens]
        + [at_dp(j) for j in dps]
    )
    for p in partners:
        pl.semaphore_signal(barrier, inc=1, device_id=p, device_id_type=MESH)
    pl.semaphore_wait(barrier, len(partners))

    ld_a.wait()
    ld_b.wait()
    swap = send(att.at[1 - core], xin, other_core)

    def dq_out(h):
        c = pl.ds(h * HW, HW)
        return (
            send(dq_a.at[:, c], dq.at[d, lo, c], at_dp(up)),
            send(dq_b.at[:, c], dq.at[d, hi, c], at_dp(dn)),
            send(dq_b.at[:, c], dq.at[d, hi, c], at_dp(up)),
            send(dq_a.at[:, c], dq.at[d, lo, c], at_dp(dn)),
        )

    def dq_forward(h, out):
        c = pl.ds(h * HW, HW)
        out[0].wait_recv()
        f = send(dq.at[dn, lo, c], dq.at[dn, lo, c], at_dp(up))
        out[1].wait_recv()
        return f, send(dq.at[up, hi, c], dq.at[up, hi, c], at_dp(dn))

    out0 = dq_out(0)
    ld_up = load(w_up, wu)
    ld_qa = load(dq_a, dq.at[d, lo])
    ld_qb = load(dq_b, dq.at[d, hi])
    ld_down = load(w_down, wd)

    swap.wait_recv()
    tot[...] = (att[core].astype(F32) + xin[...].astype(F32)).astype(BF16)
    ph1 = [send(tot.at[rows(j, BLK)], got.at[chip], at_chip(j)) for j in chips]
    got[chip] = tot[rows(chip, BLK)]

    ld_qa.wait()
    ld_qb.wait()
    ld_up.wait()
    for m in range(2):
        gnp[m] = lax.dot_general(
            dq[d, m * TOK:(m + 1) * TOK], wu[...], (((1,), (1,)), ((), ())),
            preferred_element_type=F32,
        ).astype(BF16)

    for c in ph1:
        c.wait_recv()
    run = jnp.zeros((BLK, DM), F32)
    for i in range(CH):
        j = i + core * (CH - 1 - 2 * i)
        pout[j] = run.astype(BF16)
        if i < CH - 1:
            run = run + got[j].astype(F32)
    ph2 = [send(pout.at[j], pfx.at[rows(chip, BLK)], at_chip(j)) for j in chips]
    pfx[rows(chip, BLK)] = pout[chip]
    gn = [send(gnp.at[:, rows(j, SUB)], gnr.at[k], at_tensor(j)) for k, j in enumerate(tens)]
    out1 = dq_out(1)

    for c in ph2:
        c.wait_recv()
    mine = pfx[...].astype(F32) + att[core].astype(F32)
    tot2 = xin
    tot2[...] = (mine + xin[...].astype(F32)).astype(BF16)
    back = send(tot2, hid.at[core], other_core)
    hid[core] = mine.astype(BF16)

    ld_down.wait()
    lt = []
    for m in (core, 1 - core):
        if lt:
            back.wait_recv()
        latp[m] = jnp.dot(hid[m], wd[...], preferred_element_type=F32).astype(BF16)
        lt += [
            send(latp.at[m, rows(j, SUB)], latr.at[k, m], at_tensor(j)) for k, j in enumerate(tens)
        ]

    for m in range(2):
        for q in range(4):
            for e in range(0, DSH, 64):
                at = q * DSH + e
                base = at // 128 * 128
                if at % 128 == 0 and e + 128 <= DSH:
                    htl[q, e:e + 128, m * TOK:(m + 1) * TOK] = hid[m, :, at:at + 128].T
                elif at % 128 == 0:
                    htl[q, e:e + 64, m * TOK:(m + 1) * TOK] = hid[m, :, base:base + 128].T[0:64]
                elif e == 0:
                    htl[q, 0:64, m * TOK:(m + 1) * TOK] = hid[m, :, base:base + 128].T[64:128]
    hall[d] = htl[d]
    fw0 = dq_forward(0, out0)

    for c in lt:
        c.wait_recv()

    def total(part, recv):
        x = part[:, rows(t, SUB)].astype(F32)
        for k in range(3):
            x = x + recv[k].astype(F32)
        return x.reshape(2 * SUB, QL)

    lat = total(latp, latr)
    g = gain[...].astype(F32)
    inv = lax.rsqrt(jnp.mean(lat * lat, axis=-1, keepdims=True) + EPSILON)
    nz[t] = (lat * inv * g).astype(BF16)
    an = [send(nz.at[t], nz.at[t], at_tensor(j)) for j in tens]

    def hi_lo(v):
        high = v.astype(BF16)
        low = (v - high.astype(F32)).astype(BF16)
        r = lax.broadcasted_iota(jnp.int32, (16, QL), 0)
        both = jnp.where(r == 0, high.astype(F32), jnp.where(r == 1, low.astype(F32), 0.0))
        return both.astype(BF16)

    for c in gn:
        c.wait_recv()
    gnrm = total(gnp, gnr)
    scaled = gnrm * g
    glat = inv * scaled - lat * (inv * inv * inv) * jnp.mean(scaled * lat, axis=-1, keepdims=True)
    gz[t, 0:2 * SUB] = glat.astype(BF16)
    gz[t, 2 * SUB:2 * SUB + 16] = hi_lo(jnp.sum(gnrm * lat * inv, axis=0, keepdims=True))

    fw1 = dq_forward(1, out1)

    for c in an:
        c.wait_recv()
    ag = [send(gz.at[t], gz.at[t], at_tensor(j)) for j in tens]
    for m in range(2):
        full = jnp.concatenate([nz[k, m * SUB:(m + 1) * SUB] for k in range(4)], axis=0)
        for q in range(QL // 64):
            if q % 2 == 0:
                tr = full[:, q * 64:q * 64 + 128].T
            dst, off = q * 64 // USH, q * 64 % USH
            ntl[dst, off:off + 64, m * TOK:(m + 1) * TOK] = tr[(q % 2) * 64:(q % 2) * 64 + 64]
    nt = [send(ntl.at[j], nall.at[d], at_dp(j)) for j in dps]
    nall[d] = ntl[d]
    ht = [send(htl.at[j], hall.at[d], at_dp(j)) for j in dps]

    for c in nt:
        c.wait_recv()
    ups = []
    for n in range(UCH):
        if n % (UCH // 2) == 0:
            h = n // (UCH // 2)
            for c in ((out0, out1)[h][2], (out0, out1)[h][3]) + (fw0, fw1)[h]:
                c.wait_recv()
        acc = jnp.zeros((USH, UW), F32)
        for k in range(4):
            acc = acc + jnp.dot(
                nall[k], dq[k, :, n * UW:(n + 1) * UW], preferred_element_type=F32
            )
        ubuf[n] = acc.astype(BF16)
        ups.append(send(ubuf.at[n], u_rec.at[n], mirror))
        load(ubuf.at[n], u_own.at[n])

    for c in ag:
        c.wait_recv()
    for n in range(DCH):
        for m in range(2):
            for k in range(4):
                gl[n, d, m * TOK + k * SUB:m * TOK + (k + 1) * SUB] = gz[
                    k, m * SUB:(m + 1) * SUB, n * DW:(n + 1) * DW
                ]

    def gain_rows(parts):
        v = jnp.zeros((1, QL), F32)
        for x in parts:
            v = v + jnp.sum(x.astype(F32), axis=0, keepdims=True)
        return v

    gg[d] = hi_lo(gain_rows([gz[k, 2 * SUB:2 * SUB + 16] for k in range(4)]))
    gs = [send(gg.at[d], gg.at[d], at_dp(j)) for j in dps]
    ga = [[send(gl.at[n, d], gl.at[n, d], at_dp(j)) for j in dps] for n in range(DCH)]

    for c in gs:
        c.wait_recv()
    sums = gain_rows([gg[k] for k in range(4)])
    pick = sums[:, 0:USH]
    for q in range(1, 4):
        pick = jnp.where(d == q, sums[:, q * USH:(q + 1) * USH], pick)
    gbuf[...] = jnp.broadcast_to(pick, (16, USH)).astype(BF16)
    last = [send(gbuf, g_rec, mirror)]
    load(gbuf, g_own)

    for c in ht:
        c.wait_recv()
    for n in range(DCH):
        for c in ga[n]:
            c.wait_recv()
        acc = jnp.zeros((DSH, DW), F32)
        for k in range(4):
            acc = acc + jnp.dot(hall[k], gl[n, k], preferred_element_type=F32)
        dbuf[n] = acc.astype(BF16)
        last.append(send(dbuf.at[n], d_rec.at[n], mirror))
        load(dbuf.at[n], d_own.at[n])

    for c in ups + last:
        c.wait_recv()
    for c in loads[6:]:
        c.wait()
    for c in sent:
        c.wait_send()


def finish(u_own, u_rec, d_own, d_rec, g_own, g_rec, down, gain, up):
    up[...] = (u_own[0].astype(F32) + u_rec[0].astype(F32)).astype(BF16)
    down[...] = (d_own[0].astype(F32) + d_rec[0].astype(F32)).astype(BF16)
    gain[...] = (g_own[0:1].astype(F32) + g_rec[0:1].astype(F32)).astype(BF16)


def local(attn_a, attn_b, w_down, q_gain, w_up, dq_a, dq_b):
    anywhere = pl.BlockSpec(memory_space=pl.ANY)
    vmem = pl.BlockSpec(memory_space=pltpu.VMEM)
    shapes = [
        (2, TOK, DM), (TOK, DM), (TOK, DM), (CH, BLK, DM), (CH, BLK, DM), (TOK, DM), (2, TOK, DM),
        (4, 2 * TOK, HQ), (DM, QL), (QL, HQ),
        (2, TOK, QL), (3, 2, SUB, QL), (2, TOK, QL), (3, 2, SUB, QL),
        (4, 2 * SUB, QL), (4, 2 * SUB + 16, QL),
        (4, USH, 2 * TOK), (4, USH, 2 * TOK), (DCH, 4, 2 * TOK, DW), (4, 16, QL),
        (4, DSH, 2 * TOK), (4, DSH, 2 * TOK),
        (UCH, USH, UW), (DCH, DSH, DW), (16, USH),
    ]
    halves = [(UCH, USH, UW)] * 2 + [(DCH, DSH, DW)] * 2 + [(16, USH)] * 2
    parts = pl.pallas_call(
        kernel,
        out_shape=[jax.ShapeDtypeStruct(x, BF16) for x in halves],
        in_specs=[anywhere, anywhere, anywhere, vmem, anywhere, anywhere, anywhere],
        out_specs=[anywhere] * 6,
        scratch_shapes=[pltpu.VMEM(x, BF16) for x in shapes] + [
            pltpu.SemaphoreType.DMA((16,)),
            pltpu.SemaphoreType.DMA((NCOPY,)),
            pltpu.SemaphoreType.DMA((NCOPY,)),
        ],
        compiler_params=pltpu.CompilerParams(
            collective_id=0, has_side_effects=True, vmem_limit_bytes=56 * 2**20
        ),
        name="sections",
    )(attn_a[0], attn_b[0], w_down[0], q_gain, w_up[0], dq_a[0], dq_b[0])
    ublock = pl.BlockSpec((1, USH, UW), lambda n: (n, 0, 0))
    dblock = pl.BlockSpec((1, DSH // 2, DW), lambda n: (n // 2, n % 2, 0))
    gblock = pl.BlockSpec((16, USH), lambda n: (0, 0))
    down, gain, up = pl.pallas_call(
        finish,
        grid=(4,),
        out_shape=(
            jax.ShapeDtypeStruct((DSH, QL), BF16),
            jax.ShapeDtypeStruct((1, USH), BF16),
            jax.ShapeDtypeStruct((USH, HQ), BF16),
        ),
        in_specs=[ublock, ublock, dblock, dblock, gblock, gblock],
        out_specs=(
            pl.BlockSpec((DSH // 2, DW), lambda n: (n % 2, n // 2)),
            pl.BlockSpec((1, USH), lambda n: (0, 0)),
            pl.BlockSpec((USH, UW), lambda n: (0, n)),
        ),
        compiler_params=pltpu.CompilerParams(vmem_limit_bytes=56 * 2**20),
        name="finish",
    )(*parts)
    return down[None], gain, up[None]


def solution(mesh):
    return jax.shard_map(
        local,
        mesh=mesh,
        in_specs=(
            P("section", "dp", "tensor"),
            P("section", "dp", "tensor"),
            P("section", "tensor", None),
            P("section", None),
            P("section", None, "tensor"),
            P("section", "dp", "tensor"),
            P("section", "dp", "tensor"),
        ),
        out_specs=(
            P("section", ("tensor", "dp"), None),
            P("section", "dp"),
            P("section", "dp", "tensor"),
        ),
        check_vma=False,
    )
```

```python
import functools

import jax
import jax.numpy as jnp
from jax import lax
from jax.experimental import pallas as pl
from jax.experimental.pallas import tpu as pltpu
from jax.sharding import PartitionSpec as P

EPSILON = 1e-06
MESH = pl.DeviceIdType.MESH
F32 = jnp.float32
BF16 = jnp.bfloat16

TOK = 128
DM = 1792
QL = 768
HQ = 3072
BLK = 16
SUB = TOK // 4
DSH = DM // 4
USH = QL // 4
UCH = 4
UW = HQ // UCH
DCH = 2
DW = QL // DCH
NCOPY = 96


def rows(i, n):
    return pl.ds(pl.multiple_of(i * n, n), n)


def kernel(
    attn_a, attn_b, w_down, gain, w_up, dq_a, dq_b,
    u_own, u_rec, d_own, d_rec, g_own, g_rec,
    att, xin, tot, got, pre, zout, zin, pout, pfx, hid, dq, wd, wu,
    gnp, gnr, latp, latr, nz, gz, ntl, nall, gl, gg, htl, hall,
    ubuf, dbuf, gbuf,
    lsem, ss, rs,
):
    s, t, d = lax.axis_index("section"), lax.axis_index("tensor"), lax.axis_index("dp")
    chip, core = s // 2, s % 2

    zlo, x = chip // 4, chip % 4

    def at_x(j):
        return (zlo * 8 + j * 2 + core, t, d)

    def at_tensor(j):
        return (s, j, d)

    def at_dp(j):
        return (s, t, j)

    other_core = (chip * 2 + 1 - core, t, d)
    mirror = (15 - s, t, d)
    other_row = ((s + 8) % 16, t, d)
    xs = [((x + k) % 4) for k in range(1, 4)]
    tens = [((t + k) % 4) for k in range(1, 4)]
    dps = [((d + k) % 4) for k in range(1, 4)]
    up, dn = (d + 1) % 4, (d + 3) % 4
    lo, hi = pl.ds(0, TOK), pl.ds(TOK, TOK)

    counter = [0]
    sent = []

    def send(src, dst, to):
        i = counter[0]
        counter[0] += 1
        copy = pltpu.make_async_remote_copy(
            src_ref=src, dst_ref=dst, send_sem=ss.at[i], recv_sem=rs.at[i],
            device_id=to, device_id_type=MESH,
        )
        copy.start()
        sent.append(copy)
        return copy

    loads = []

    def load(src, dst):
        c = pltpu.make_async_copy(src, dst, lsem.at[len(loads)])
        c.start()
        loads.append(c)
        return c

    ld_a = load(attn_a, att.at[0])
    ld_b = load(attn_b, att.at[1])

    barrier = pltpu.get_barrier_semaphore()
    partners = (
        [other_core, mirror, other_row]
        + [at_x(j) for j in xs]
        + [at_tensor(j) for j in tens]
        + [at_dp(j) for j in dps]
    )
    for p in partners:
        pl.semaphore_signal(barrier, inc=1, device_id=p, device_id_type=MESH)
    pl.semaphore_wait(barrier, len(partners))

    def dq_out(h):
        c = pl.ds(h * UW, UW)
        return (
            send(dq_a.at[:, c], dq.at[d, lo, c], at_dp(up)),
            send(dq_b.at[:, c], dq.at[d, hi, c], at_dp(dn)),
            send(dq_b.at[:, c], dq.at[d, hi, c], at_dp(up)),
            send(dq_a.at[:, c], dq.at[d, lo, c], at_dp(dn)),
        )

    def dq_forward(h):
        c = pl.ds(h * UW, UW)
        out[h][0].wait_recv()
        f = send(dq.at[dn, lo, c], dq.at[dn, lo, c], at_dp(up))
        out[h][1].wait_recv()
        return f, send(dq.at[up, hi, c], dq.at[up, hi, c], at_dp(dn))

    ld_a.wait()
    ld_b.wait()
    swap = send(att.at[1 - core], xin, other_core)
    out = [dq_out(0), dq_out(1)]
    ld_qa = load(dq_a, dq.at[d, lo])
    ld_qb = load(dq_b, dq.at[d, hi])
    ld_up = load(w_up, wu)
    ld_down = load(w_down, wd)

    swap.wait_recv()
    tot[...] = (att[core].astype(F32) + xin[...].astype(F32)).astype(BF16)
    ph1 = []
    for h in range(2):
        ph1.append([send(tot.at[rows(j * 2 + h, BLK)], got.at[h, x], at_x(j)) for j in xs])
        got[h, x] = tot[rows(x * 2 + h, BLK)]

    ld_qa.wait()
    ld_qb.wait()
    ld_up.wait()
    for m in range(2):
        gnp[m] = lax.dot_general(
            dq[d, m * TOK:(m + 1) * TOK], wu[...], (((1,), (1,)), ((), ())),
            preferred_element_type=F32,
        ).astype(BF16)

    totals = []
    for h in range(2):
        for c in ph1[h]:
            c.wait_recv()
        run = jnp.zeros((BLK, DM), F32)
        for i in range(4):
            j = i + core * (3 - 2 * i)
            pre[h, j] = run
            run = run + got[h, j].astype(F32)
        zout[h] = run.astype(BF16)
        totals.append(send(zout.at[h], zin.at[h], other_row))

    gn = [send(gnp.at[:, rows(j, SUB)], gnr.at[k], at_tensor(j)) for k, j in enumerate(tens)]
    out.append(dq_out(2))

    ph2 = []
    behind = zlo + core == 1
    for h in range(2):
        totals[h].wait_recv()
        far = jnp.where(behind, zin[h].astype(F32), 0.0)
        for j in range(4):
            pout[h, j] = (pre[h, j] + far).astype(BF16)
        ph2 += [send(pout.at[h, j], pfx.at[rows(x * 2 + h, BLK)], at_x(j)) for j in xs]
        pfx[rows(x * 2 + h, BLK)] = pout[h, x]
    out.append(dq_out(3))
    fw = [dq_forward(0)]

    for c in ph2:
        c.wait_recv()
    mine = pfx[...].astype(F32) + att[core].astype(F32)
    tot2 = xin
    tot2[...] = (mine + xin[...].astype(F32)).astype(BF16)
    back = send(tot2, hid.at[core], other_core)
    hid[core] = mine.astype(BF16)

    ld_down.wait()
    lt = []
    for m in (core, 1 - core):
        if lt:
            back.wait_recv()
        latp[m] = jnp.dot(hid[m], wd[...], preferred_element_type=F32).astype(BF16)
        lt.append([
            send(latp.at[m, rows(j, SUB)], latr.at[k, m], at_tensor(j)) for k, j in enumerate(tens)
        ])
    fw.append(dq_forward(1))

    for m in range(2):
        for q in range(4):
            for e in range(0, DSH, 64):
                at = q * DSH + e
                base = at // 128 * 128
                if at % 128 == 0 and e + 128 <= DSH:
                    htl[q, e:e + 128, m * TOK:(m + 1) * TOK] = hid[m, :, at:at + 128].T
                elif at % 128 == 0:
                    htl[q, e:e + 64, m * TOK:(m + 1) * TOK] = hid[m, :, base:base + 128].T[0:64]
                elif e == 0:
                    htl[q, 0:64, m * TOK:(m + 1) * TOK] = hid[m, :, base:base + 128].T[64:128]
    hall[d] = htl[d]

    def total(part, recv, m):
        v = part[m, rows(t, SUB)].astype(F32)
        for k in range(3):
            v = v + recv[k, m].astype(F32)
        return v

    g = gain[...].astype(F32)
    an = []
    for n, m in enumerate((core, 1 - core)):
        for c in lt[n]:
            c.wait_recv()
        lat = total(latp, latr, m)
        inv = lax.rsqrt(jnp.mean(lat * lat, axis=-1, keepdims=True) + EPSILON)
        nz[t, m] = (lat * inv * g).astype(BF16)
        an.append([send(nz.at[t, m], nz.at[t, m], at_tensor(j)) for j in tens])

    def hi_lo(v):
        high = v.astype(BF16)
        low = (v - high.astype(F32)).astype(BF16)
        r = lax.broadcasted_iota(jnp.int32, (16, QL), 0)
        both = jnp.where(r == 0, high.astype(F32), jnp.where(r == 1, low.astype(F32), 0.0))
        return both.astype(BF16)

    for c in gn:
        c.wait_recv()
    part = jnp.zeros((1, QL), F32)
    for m in range(2):
        lat = total(latp, latr, m)
        inv = lax.rsqrt(jnp.mean(lat * lat, axis=-1, keepdims=True) + EPSILON)
        gnrm = total(gnp, gnr, m)
        scaled = gnrm * g
        back_mean = jnp.mean(scaled * lat, axis=-1, keepdims=True)
        gz[t, m * SUB:(m + 1) * SUB] = (
            inv * scaled - lat * (inv * inv * inv) * back_mean
        ).astype(BF16)
        part = part + jnp.sum(gnrm * lat * inv, axis=0, keepdims=True)
    gz[t, 2 * SUB:2 * SUB + 16] = hi_lo(part)

    for n, m in enumerate((core, 1 - core)):
        for c in an[n]:
            c.wait_recv()
        if n == 1:
            ag = [send(gz.at[t], gz.at[t], at_tensor(j)) for j in tens]
        full = jnp.concatenate([nz[k, m] for k in range(4)], axis=0)
        lanes = pl.ds(pl.multiple_of(m * TOK, TOK), TOK)
        for q in range(QL // 64):
            if q % 2 == 0:
                tr = full[:, q * 64:q * 64 + 128].T
            dst, off = q * 64 // USH, q * 64 % USH
            ntl[dst, off:off + 64, lanes] = tr[(q % 2) * 64:(q % 2) * 64 + 64]
    nt = [send(ntl.at[j], nall.at[d], at_dp(j)) for j in dps]
    nall[d] = ntl[d]
    fw.append(dq_forward(2))
    fw.append(dq_forward(3))

    for c in nt:
        c.wait_recv()
    ups = []

    def grad_up(n):
        for c in (out[n][2], out[n][3]) + fw[n]:
            c.wait_recv()
        acc = jnp.zeros((USH, UW), F32)
        for k in range(4):
            acc = acc + jnp.dot(
                nall[k], dq[k, :, n * UW:(n + 1) * UW], preferred_element_type=F32
            )
        ubuf[n] = acc.astype(BF16)
        ups.append(send(ubuf.at[n], u_rec.at[n], mirror))
        load(ubuf.at[n], u_own.at[n])

    grad_up(0)
    grad_up(1)

    for c in ag:
        c.wait_recv()
    for n in range(DCH):
        for m in range(2):
            for k in range(4):
                gl[n, d, m * TOK + k * SUB:m * TOK + (k + 1) * SUB] = gz[
                    k, m * SUB:(m + 1) * SUB, n * DW:(n + 1) * DW
                ]

    def gain_rows(parts):
        v = jnp.zeros((1, QL), F32)
        for p in parts:
            v = v + jnp.sum(p.astype(F32), axis=0, keepdims=True)
        return v

    gg[d] = hi_lo(gain_rows([gz[k, 2 * SUB:2 * SUB + 16] for k in range(4)]))
    ga = [[
        send(gl.at[n, d, r], gl.at[n, d, r], at_dp(j))
        for r, j in ((lo, up), (hi, dn), (hi, up), (lo, dn))
    ] for n in range(DCH)]
    gs = [send(gg.at[d], gg.at[d], at_dp(j)) for j in dps]
    ht = [send(htl.at[j], hall.at[d], at_dp(j)) for j in dps]
    grad_up(2)
    grad_up(3)

    for n in range(DCH):
        ga[n][0].wait_recv()
        ga[n].append(send(gl.at[n, dn, lo], gl.at[n, dn, lo], at_dp(up)))
        ga[n][1].wait_recv()
        ga[n].append(send(gl.at[n, up, hi], gl.at[n, up, hi], at_dp(dn)))

    for c in gs:
        c.wait_recv()
    sums = gain_rows([gg[k] for k in range(4)])
    pick = sums[:, 0:USH]
    for q in range(1, 4):
        pick = jnp.where(d == q, sums[:, q * USH:(q + 1) * USH], pick)
    gbuf[...] = jnp.broadcast_to(pick, (16, USH)).astype(BF16)
    last = [send(gbuf, g_rec, mirror)]
    load(gbuf, g_own)

    for c in ht:
        c.wait_recv()
    for n in range(DCH):
        for c in ga[n][2:]:
            c.wait_recv()
        acc = jnp.zeros((DSH, DW), F32)
        for k in range(4):
            acc = acc + jnp.dot(hall[k], gl[n, k], preferred_element_type=F32)
        dbuf[n] = acc.astype(BF16)
        last.append(send(dbuf.at[n], d_rec.at[n], mirror))
        load(dbuf.at[n], d_own.at[n])

    for c in ups + last:
        c.wait_recv()
    for c in loads[6:]:
        c.wait()
    for c in sent:
        c.wait_send()


def finish(u_own, u_rec, d_own, d_rec, g_own, g_rec, down, gain, up):
    up[...] = (u_own[0].astype(F32) + u_rec[0].astype(F32)).astype(BF16)
    down[...] = (d_own[0].astype(F32) + d_rec[0].astype(F32)).astype(BF16)
    gain[...] = (g_own[0:1].astype(F32) + g_rec[0:1].astype(F32)).astype(BF16)


def local(attn_a, attn_b, w_down, q_gain, w_up, dq_a, dq_b):
    anywhere = pl.BlockSpec(memory_space=pl.ANY)
    vmem = pl.BlockSpec(memory_space=pltpu.VMEM)
    shapes = [
        (2, TOK, DM), (TOK, DM), (TOK, DM), (2, 4, BLK, DM), (2, 4, BLK, DM), (2, BLK, DM),
        (2, BLK, DM), (2, 4, BLK, DM), (TOK, DM), (2, TOK, DM),
        (4, 2 * TOK, HQ), (DM, QL), (QL, HQ),
        (2, TOK, QL), (3, 2, SUB, QL), (2, TOK, QL), (3, 2, SUB, QL),
        (4, 2, SUB, QL), (4, 2 * SUB + 16, QL),
        (4, USH, 2 * TOK), (4, USH, 2 * TOK), (DCH, 4, 2 * TOK, DW), (4, 16, QL),
        (4, DSH, 2 * TOK), (4, DSH, 2 * TOK),
        (UCH, USH, UW), (DCH, DSH, DW), (16, USH),
    ]
    halves = [(UCH, USH, UW)] * 2 + [(DCH, DSH, DW)] * 2 + [(16, USH)] * 2
    parts = pl.pallas_call(
        kernel,
        out_shape=[jax.ShapeDtypeStruct(x, BF16) for x in halves],
        in_specs=[anywhere, anywhere, anywhere, vmem, anywhere, anywhere, anywhere],
        out_specs=[anywhere] * 6,
        scratch_shapes=[pltpu.VMEM(x, F32 if i == 4 else BF16) for i, x in enumerate(shapes)] + [
            pltpu.SemaphoreType.DMA((16,)),
            pltpu.SemaphoreType.DMA((NCOPY,)),
            pltpu.SemaphoreType.DMA((NCOPY,)),
        ],
        compiler_params=pltpu.CompilerParams(
            collective_id=0, has_side_effects=True, vmem_limit_bytes=56 * 2**20
        ),
        name="sections",
    )(attn_a[0], attn_b[0], w_down[0], q_gain, w_up[0], dq_a[0], dq_b[0])
    ublock = pl.BlockSpec((1, USH, UW), lambda n: (n, 0, 0))
    dblock = pl.BlockSpec((1, DSH // 2, DW), lambda n: (n // 2, n % 2, 0))
    gblock = pl.BlockSpec((16, USH), lambda n: (0, 0))
    down, gain, up = pl.pallas_call(
        finish,
        grid=(4,),
        out_shape=(
            jax.ShapeDtypeStruct((DSH, QL), BF16),
            jax.ShapeDtypeStruct((1, USH), BF16),
            jax.ShapeDtypeStruct((USH, HQ), BF16),
        ),
        in_specs=[ublock, ublock, dblock, dblock, gblock, gblock],
        out_specs=(
            pl.BlockSpec((DSH // 2, DW), lambda n: (n % 2, n // 2)),
            pl.BlockSpec((1, USH), lambda n: (0, 0)),
            pl.BlockSpec((USH, UW), lambda n: (0, n)),
        ),
        compiler_params=pltpu.CompilerParams(vmem_limit_bytes=56 * 2**20),
        name="finish",
    )(*parts)
    return down[None], gain, up[None]


def solution(mesh):
    return jax.shard_map(
        local,
        mesh=mesh,
        in_specs=(
            P("section", "dp", "tensor"),
            P("section", "dp", "tensor"),
            P("section", "tensor", None),
            P("section", None),
            P("section", None, "tensor"),
            P("section", "dp", "tensor"),
            P("section", "dp", "tensor"),
        ),
        out_specs=(
            P("section", ("tensor", "dp"), None),
            P("section", "dp"),
            P("section", "dp", "tensor"),
        ),
        check_vma=False,
    )
```

```python
import functools

import jax
import jax.numpy as jnp
from jax import lax
from jax.experimental import pallas as pl
from jax.experimental.pallas import tpu as pltpu
from jax.sharding import PartitionSpec as P

EPSILON = 1e-06
MESH = pl.DeviceIdType.MESH
F32 = jnp.float32
BF16 = jnp.bfloat16

TOK = 128
DM = 1792
QL = 768
HQ = 3072
BLK = 16
SUB = TOK // 4
DSH = DM // 4
USH = QL // 4
UCH = 4
UW = HQ // UCH
DCOLS = ((0, 384), (384, 256), (640, 128))
NCOPY = 128
STEPS = 2


def rows(i, n):
    return pl.ds(pl.multiple_of(i * n, n), n)


def kernel(
    attn_a, attn_b, w_down, gain, w_up, dq_a, dq_b,
    u_own, u_rec, d_own, d_rec, g_own, g_rec,
    att, xin, tot, got, pre, zout, zin, pout, pfx, hid, dq, wd, wu,
    gnp, gnr, latp, latr, nz, gz, ntl, nall, gl, gg, htl, hall,
    ubuf, dbuf, gbuf,
    lsem, ss, rs,
):
    s, t, d = lax.axis_index("section"), lax.axis_index("tensor"), lax.axis_index("dp")
    chip, core = s // 2, s % 2

    zlo, x = chip // 4, chip % 4

    def at_x(j):
        return (zlo * 8 + j * 2 + core, t, d)

    def at_tensor(j):
        return (s, j, d)

    def at_dp(j):
        return (s, t, j)

    other_core = (chip * 2 + 1 - core, t, d)
    mirror = (15 - s, t, d)
    other_row = ((s + 8) % 16, t, d)
    xs = [((x + k) % 4) for k in range(1, 4)]
    tens = [((t + k) % 4) for k in range(1, 4)]
    dps = [((d + k) % 4) for k in range(1, 4)]
    up, dn = (d + 1) % 4, (d + 3) % 4
    lo, hi = pl.ds(0, TOK), pl.ds(TOK, TOK)

    counter = [0]
    sent = []

    def send(src, dst, to):
        i = counter[0]
        counter[0] += 1
        assert i < NCOPY
        copy = pltpu.make_async_remote_copy(
            src_ref=src, dst_ref=dst, send_sem=ss.at[i], recv_sem=rs.at[i],
            device_id=to, device_id_type=MESH,
        )
        copy.start()
        sent.append(copy)
        return copy

    loads = []

    def load(src, dst):
        c = pltpu.make_async_copy(src, dst, lsem.at[len(loads)])
        c.start()
        loads.append(c)
        return c

    ld_a = load(attn_a, att.at[0])
    ld_b = load(attn_b, att.at[1])

    barrier = pltpu.get_barrier_semaphore()
    partners = (
        [other_core, mirror, other_row]
        + [at_x(j) for j in xs]
        + [at_tensor(j) for j in tens]
        + [at_dp(j) for j in dps]
    )
    for p in partners:
        pl.semaphore_signal(barrier, inc=1, device_id=p, device_id_type=MESH)
    pl.semaphore_wait(barrier, len(partners))

    def dq_out(h):
        c = pl.ds(h * UW, UW)
        return (
            send(dq_a.at[:, c], dq.at[d, lo, c], at_dp(up)),
            send(dq_b.at[:, c], dq.at[d, hi, c], at_dp(dn)),
            send(dq_b.at[:, c], dq.at[d, hi, c], at_dp(up)),
            send(dq_a.at[:, c], dq.at[d, lo, c], at_dp(dn)),
        )

    def dq_forward(h):
        c = pl.ds(h * UW, UW)
        out[h][0].wait_recv()
        f = send(dq.at[dn, lo, c], dq.at[dn, lo, c], at_dp(up))
        out[h][1].wait_recv()
        return f, send(dq.at[up, hi, c], dq.at[up, hi, c], at_dp(dn))

    ld_a.wait()
    ld_b.wait()
    swap = send(att.at[1 - core], xin, other_core)
    out = [dq_out(0), dq_out(1)]
    ld_qa = load(dq_a, dq.at[d, lo])
    ld_qb = load(dq_b, dq.at[d, hi])
    ld_up = load(w_up, wu)
    ld_down = load(w_down, wd)

    swap.wait_recv()
    tot[...] = (att[core].astype(F32) + xin[...].astype(F32)).astype(BF16)
    ph1 = []
    for h in range(2):
        ph1.append([send(tot.at[rows(j * 2 + h, BLK)], got.at[h, x], at_x(j)) for j in xs])
        got[h, x] = tot[rows(x * 2 + h, BLK)]

    ld_qa.wait()
    ld_qb.wait()
    ld_up.wait()
    for m in range(2):
        gnp[m] = lax.dot_general(
            dq[d, m * TOK:(m + 1) * TOK], wu[...], (((1,), (1,)), ((), ())),
            preferred_element_type=F32,
        ).astype(BF16)

    totals = []
    for h in range(2):
        for c in ph1[h]:
            c.wait_recv()
        run = jnp.zeros((BLK, DM), F32)
        for i in range(4):
            j = i + core * (3 - 2 * i)
            pre[h, j] = run
            run = run + got[h, j].astype(F32)
        zout[h] = run.astype(BF16)
        totals.append(send(zout.at[h], zin.at[h], other_row))

    gn = [send(gnp.at[:, rows(j, SUB)], gnr.at[k], at_tensor(j)) for k, j in enumerate(tens)]
    out.append(dq_out(2))

    ph2 = []
    behind = zlo + core == 1
    for h in range(2):
        totals[h].wait_recv()
        far = jnp.where(behind, zin[h].astype(F32), 0.0)
        for j in range(4):
            pout[h, j] = (pre[h, j] + far).astype(BF16)
        ph2 += [send(pout.at[h, j], pfx.at[rows(x * 2 + h, BLK)], at_x(j)) for j in xs]
        pfx[rows(x * 2 + h, BLK)] = pout[h, x]
    out.append(dq_out(3))
    fw = [dq_forward(0)]

    for c in ph2:
        c.wait_recv()
    mine = pfx[...].astype(F32) + att[core].astype(F32)
    tot2 = xin
    tot2[...] = (mine + xin[...].astype(F32)).astype(BF16)
    back = send(tot2, hid.at[core], other_core)
    hid[core] = mine.astype(BF16)

    ld_down.wait()
    lt = []
    for m in (core, 1 - core):
        if lt:
            back.wait_recv()
        latp[m] = jnp.dot(hid[m], wd[...], preferred_element_type=F32).astype(BF16)
        lt.append([
            send(latp.at[m, rows(j, SUB)], latr.at[k, m], at_tensor(j)) for k, j in enumerate(tens)
        ])
    fw.append(dq_forward(1))

    for m in range(2):
        for q in range(4):
            for e in range(0, DSH, 64):
                at = q * DSH + e
                base = at // 128 * 128
                if at % 128 == 0 and e + 128 <= DSH:
                    htl[q, e:e + 128, m * TOK:(m + 1) * TOK] = hid[m, :, at:at + 128].T
                elif at % 128 == 0:
                    htl[q, e:e + 64, m * TOK:(m + 1) * TOK] = hid[m, :, base:base + 128].T[0:64]
                elif e == 0:
                    htl[q, 0:64, m * TOK:(m + 1) * TOK] = hid[m, :, base:base + 128].T[64:128]
    hall[d] = htl[d]

    def total(part, recv, m):
        v = part[m, rows(t, SUB)].astype(F32)
        for k in range(3):
            v = v + recv[k, m].astype(F32)
        return v

    g = gain[...].astype(F32)
    an = []
    for n, m in enumerate((core, 1 - core)):
        for c in lt[n]:
            c.wait_recv()
        lat = total(latp, latr, m)
        inv = lax.rsqrt(jnp.mean(lat * lat, axis=-1, keepdims=True) + EPSILON)
        nz[t, m] = (lat * inv * g).astype(BF16)
        an.append([send(nz.at[t, m], nz.at[t, m], at_tensor(j)) for j in tens])

    def hi_lo(v):
        high = v.astype(BF16)
        low = (v - high.astype(F32)).astype(BF16)
        r = lax.broadcasted_iota(jnp.int32, (16, QL), 0)
        both = jnp.where(r == 0, high.astype(F32), jnp.where(r == 1, low.astype(F32), 0.0))
        return both.astype(BF16)

    for c in gn:
        c.wait_recv()
    part = jnp.zeros((1, QL), F32)
    for m in range(2):
        lat = total(latp, latr, m)
        inv = lax.rsqrt(jnp.mean(lat * lat, axis=-1, keepdims=True) + EPSILON)
        gnrm = total(gnp, gnr, m)
        scaled = gnrm * g
        back_mean = jnp.mean(scaled * lat, axis=-1, keepdims=True)
        gz[t, m * SUB:(m + 1) * SUB] = (
            inv * scaled - lat * (inv * inv * inv) * back_mean
        ).astype(BF16)
        part = part + jnp.sum(gnrm * lat * inv, axis=0, keepdims=True)
    gz[t, 2 * SUB:2 * SUB + 16] = hi_lo(part)

    for n, m in enumerate((core, 1 - core)):
        for c in an[n]:
            c.wait_recv()
        if n == 1:
            ag = [send(gz.at[t], gz.at[t], at_tensor(j)) for j in tens]
        full = jnp.concatenate([nz[k, m] for k in range(4)], axis=0)
        lanes = pl.ds(pl.multiple_of(m * TOK, TOK), TOK)
        for q in range(QL // 64):
            if q % 2 == 0:
                tr = full[:, q * 64:q * 64 + 128].T
            dst, off = q * 64 // USH, q * 64 % USH
            ntl[dst, off:off + 64, lanes] = tr[(q % 2) * 64:(q % 2) * 64 + 64]
    nt = [send(ntl.at[j], nall.at[d], at_dp(j)) for j in dps]
    nall[d] = ntl[d]

    for c in nt:
        c.wait_recv()
    ups = []

    def grad_up(n):
        for c in (out[n][2], out[n][3]) + fw[n]:
            c.wait_recv()
        acc = jnp.zeros((USH, UW), F32)
        for k in range(4):
            acc = acc + jnp.dot(
                nall[k], dq[k, :, n * UW:(n + 1) * UW], preferred_element_type=F32
            )
        ubuf[n] = acc.astype(BF16)
        ups.append(send(ubuf.at[n], u_rec.at[n], mirror))
        load(ubuf.at[n], u_own.at[n])

    fw.append(dq_forward(2))
    grad_up(0)
    fw.append(dq_forward(3))
    grad_up(1)

    for c in ag:
        c.wait_recv()
    for m in range(2):
        for k in range(4):
            gl[d, m * TOK + k * SUB:m * TOK + (k + 1) * SUB] = gz[k, m * SUB:(m + 1) * SUB]

    def gain_rows(parts):
        v = jnp.zeros((1, QL), F32)
        for p in parts:
            v = v + jnp.sum(p.astype(F32), axis=0, keepdims=True)
        return v

    gg[d] = hi_lo(gain_rows([gz[k, 2 * SUB:2 * SUB + 16] for k in range(4)]))
    ga = []

    def cols(n):
        return pl.ds(*DCOLS[n])

    def gl_out(n):
        ga.append([
            send(gl.at[d, r, cols(n)], gl.at[d, r, cols(n)], at_dp(j))
            for r, j in ((lo, up), (hi, dn), (hi, up), (lo, dn))
        ])

    gl_out(0)
    gl_out(1)
    gs = [send(gg.at[d], gg.at[d], at_dp(j)) for j in dps]
    ht = [send(htl.at[j], hall.at[d], at_dp(j)) for j in dps]
    grad_up(2)
    grad_up(3)

    def gl_forward(n):
        ga[n][0].wait_recv()
        ga[n].append(send(gl.at[dn, lo, cols(n)], gl.at[dn, lo, cols(n)], at_dp(up)))
        ga[n][1].wait_recv()
        ga[n].append(send(gl.at[up, hi, cols(n)], gl.at[up, hi, cols(n)], at_dp(dn)))

    gl_forward(0)
    gl_out(2)
    gl_forward(1)

    for c in gs:
        c.wait_recv()
    sums = gain_rows([gg[k] for k in range(4)])
    pick = sums[:, 0:USH]
    for q in range(1, 4):
        pick = jnp.where(d == q, sums[:, q * USH:(q + 1) * USH], pick)
    gbuf[...] = jnp.broadcast_to(pick, (16, USH)).astype(BF16)
    last = [send(gbuf, g_rec, mirror)]
    load(gbuf, g_own)

    for c in ht:
        c.wait_recv()
    for n in range(len(DCOLS)):
        if n == 1:
            gl_forward(2)
        for c in ga[n][2:]:
            c.wait_recv()
        acc = jnp.zeros((DSH, DCOLS[n][1]), F32)
        for k in range(4):
            acc = acc + jnp.dot(hall[k], gl[k, :, cols(n)], preferred_element_type=F32)
        dbuf[:, cols(n)] = acc.astype(BF16)
        last.append(send(dbuf.at[:, cols(n)], d_rec.at[:, cols(n)], mirror))
        load(dbuf.at[:, cols(n)], d_own.at[:, cols(n)])

    for c in ups + last:
        c.wait_recv()
    for c in loads[6:]:
        c.wait()
    for c in sent:
        c.wait_send()


def finish(u_own, u_rec, d_own, d_rec, g_own, g_rec, down, gain, up):
    for n in range(UCH // STEPS):
        both = u_own[n].astype(F32) + u_rec[n].astype(F32)
        up[:, n * UW:(n + 1) * UW] = both.astype(BF16)
    down[...] = (d_own[...].astype(F32) + d_rec[...].astype(F32)).astype(BF16)
    gain[...] = (g_own[0:1].astype(F32) + g_rec[0:1].astype(F32)).astype(BF16)


def local(attn_a, attn_b, w_down, q_gain, w_up, dq_a, dq_b):
    anywhere = pl.BlockSpec(memory_space=pl.ANY)
    vmem = pl.BlockSpec(memory_space=pltpu.VMEM)
    shapes = [
        (2, TOK, DM), (TOK, DM), (TOK, DM), (2, 4, BLK, DM), (2, 4, BLK, DM), (2, BLK, DM),
        (2, BLK, DM), (2, 4, BLK, DM), (TOK, DM), (2, TOK, DM),
        (4, 2 * TOK, HQ), (DM, QL), (QL, HQ),
        (2, TOK, QL), (3, 2, SUB, QL), (2, TOK, QL), (3, 2, SUB, QL),
        (4, 2, SUB, QL), (4, 2 * SUB + 16, QL),
        (4, USH, 2 * TOK), (4, USH, 2 * TOK), (4, 2 * TOK, QL), (4, 16, QL),
        (4, DSH, 2 * TOK), (4, DSH, 2 * TOK),
        (UCH, USH, UW), (DSH, QL), (16, USH),
    ]
    halves = [(UCH, USH, UW)] * 2 + [(DSH, QL)] * 2 + [(16, USH)] * 2
    parts = pl.pallas_call(
        kernel,
        out_shape=[jax.ShapeDtypeStruct(x, BF16) for x in halves],
        in_specs=[anywhere, anywhere, anywhere, vmem, anywhere, anywhere, anywhere],
        out_specs=[anywhere] * 6,
        scratch_shapes=[pltpu.VMEM(x, F32 if i == 4 else BF16) for i, x in enumerate(shapes)] + [
            pltpu.SemaphoreType.DMA((16,)),
            pltpu.SemaphoreType.DMA((NCOPY,)),
            pltpu.SemaphoreType.DMA((NCOPY,)),
        ],
        compiler_params=pltpu.CompilerParams(
            collective_id=0, has_side_effects=True, vmem_limit_bytes=56 * 2**20
        ),
        name="sections",
    )(attn_a[0], attn_b[0], w_down[0], q_gain, w_up[0], dq_a[0], dq_b[0])
    ublock = pl.BlockSpec((UCH // STEPS, USH, UW), lambda n: (n, 0, 0))
    dblock = pl.BlockSpec((DSH // STEPS, QL), lambda n: (n, 0))
    gblock = pl.BlockSpec((16, USH), lambda n: (0, 0))
    down, gain, up = pl.pallas_call(
        finish,
        grid=(STEPS,),
        out_shape=(
            jax.ShapeDtypeStruct((DSH, QL), BF16),
            jax.ShapeDtypeStruct((1, USH), BF16),
            jax.ShapeDtypeStruct((USH, HQ), BF16),
        ),
        in_specs=[ublock, ublock, dblock, dblock, gblock, gblock],
        out_specs=(
            dblock,
            pl.BlockSpec((1, USH), lambda n: (0, 0)),
            pl.BlockSpec((USH, HQ // STEPS), lambda n: (0, n)),
        ),
        compiler_params=pltpu.CompilerParams(vmem_limit_bytes=56 * 2**20),
        name="finish",
    )(*parts)
    return down[None], gain, up[None]


def solution(mesh):
    return jax.shard_map(
        local,
        mesh=mesh,
        in_specs=(
            P("section", "dp", "tensor"),
            P("section", "dp", "tensor"),
            P("section", "tensor", None),
            P("section", None),
            P("section", None, "tensor"),
            P("section", "dp", "tensor"),
            P("section", "dp", "tensor"),
        ),
        out_specs=(
            P("section", ("tensor", "dp"), None),
            P("section", "dp"),
            P("section", "dp", "tensor"),
        ),
        check_vma=False,
    )
```

```python
import functools

import jax
import jax.numpy as jnp
from jax import lax
from jax.experimental import pallas as pl
from jax.experimental.pallas import tpu as pltpu
from jax.sharding import PartitionSpec as P

EPSILON = 1e-06
MESH = pl.DeviceIdType.MESH
F32 = jnp.float32
BF16 = jnp.bfloat16

TOK = 128
DM = 1792
QL = 768
HQ = 3072
BLK = 16
SUB = TOK // 4
DSH = DM // 4
USH = QL // 4
UCH = 4
UW = HQ // UCH
DCOLS = ((0, 384), (384, 256), (640, 128))
NCOPY = 128
STEPS = 2


def rows(i, n):
    return pl.ds(pl.multiple_of(i * n, n), n)


def kernel(
    attn_a, attn_b, w_down, gain, w_up, dq_a, dq_b,
    u_own, u_rec, d_own, d_rec, g_own, g_rec,
    att, xin, tot, got, pre, zout, zin, pout, pfx, hid, dq, wd, wu,
    gnp, gnr, latp, latr, nz, gz, gp, ntl, nall, gl, gg, htl, hall,
    ubuf, dbuf, gbuf,
    lsem, ss, rs,
):
    s, t, d = lax.axis_index("section"), lax.axis_index("tensor"), lax.axis_index("dp")
    chip, core = s // 2, s % 2

    zlo, x = chip // 4, chip % 4

    def at_x(j):
        return (zlo * 8 + j * 2 + core, t, d)

    def at_tensor(j):
        return (s, j, d)

    def at_dp(j):
        return (s, t, j)

    other_core = (chip * 2 + 1 - core, t, d)
    mirror = (15 - s, t, d)
    other_row = ((s + 8) % 16, t, d)
    xs = [((x + k) % 4) for k in range(1, 4)]
    tens = [((t + k) % 4) for k in range(1, 4)]
    dps = [((d + k) % 4) for k in range(1, 4)]
    up, dn = (d + 1) % 4, (d + 3) % 4
    lo, hi = pl.ds(0, TOK), pl.ds(TOK, TOK)

    counter = [0]
    sent = []

    def send(src, dst, to):
        i = counter[0]
        counter[0] += 1
        assert i < NCOPY
        copy = pltpu.make_async_remote_copy(
            src_ref=src, dst_ref=dst, send_sem=ss.at[i], recv_sem=rs.at[i],
            device_id=to, device_id_type=MESH,
        )
        copy.start()
        sent.append(copy)
        return copy

    loads = []

    def load(src, dst):
        c = pltpu.make_async_copy(src, dst, lsem.at[len(loads)])
        c.start()
        loads.append(c)
        return c

    ld_a = load(attn_a, att.at[0])
    ld_b = load(attn_b, att.at[1])

    barrier = pltpu.get_barrier_semaphore()
    partners = (
        [other_core, mirror, other_row]
        + [at_x(j) for j in xs]
        + [at_tensor(j) for j in tens]
        + [at_dp(j) for j in dps]
    )
    for p in partners:
        pl.semaphore_signal(barrier, inc=1, device_id=p, device_id_type=MESH)
    pl.semaphore_wait(barrier, len(partners))

    def dq_out(h):
        c = pl.ds(h * UW, UW)
        return (
            send(dq_a.at[:, c], dq.at[d, lo, c], at_dp(up)),
            send(dq_b.at[:, c], dq.at[d, hi, c], at_dp(dn)),
            send(dq_b.at[:, c], dq.at[d, hi, c], at_dp(up)),
            send(dq_a.at[:, c], dq.at[d, lo, c], at_dp(dn)),
        )

    def dq_forward(h):
        c = pl.ds(h * UW, UW)
        out[h][0].wait_recv()
        f = send(dq.at[dn, lo, c], dq.at[dn, lo, c], at_dp(up))
        out[h][1].wait_recv()
        return f, send(dq.at[up, hi, c], dq.at[up, hi, c], at_dp(dn))

    ld_a.wait()
    ld_b.wait()
    swap = send(att.at[1 - core], xin, other_core)
    out = [dq_out(0), dq_out(1)]
    ld_qa = load(dq_a, dq.at[d, lo])
    ld_qb = load(dq_b, dq.at[d, hi])
    ld_up = load(w_up, wu)
    ld_down = load(w_down, wd)

    swap.wait_recv()
    tot[...] = (att[core].astype(F32) + xin[...].astype(F32)).astype(BF16)
    ph1 = []
    for h in range(2):
        ph1.append([send(tot.at[rows(j * 2 + h, BLK)], got.at[h, x], at_x(j)) for j in xs])
        got[h, x] = tot[rows(x * 2 + h, BLK)]

    ld_qa.wait()
    ld_qb.wait()
    ld_up.wait()
    for m in range(2):
        gnp[m] = lax.dot_general(
            dq[d, m * TOK:(m + 1) * TOK], wu[...], (((1,), (1,)), ((), ())),
            preferred_element_type=F32,
        ).astype(BF16)

    totals = []
    for h in range(2):
        for c in ph1[h]:
            c.wait_recv()
        run = jnp.zeros((BLK, DM), F32)
        for i in range(4):
            j = i + core * (3 - 2 * i)
            pre[h, j] = run
            run = run + got[h, j].astype(F32)
        zout[h] = run.astype(BF16)
        totals.append(send(zout.at[h], zin.at[h], other_row))

    gn = [send(gnp.at[:, rows(j, SUB)], gnr.at[k], at_tensor(j)) for k, j in enumerate(tens)]
    out.append(dq_out(2))

    ph2 = []
    behind = zlo + core == 1
    for h in range(2):
        totals[h].wait_recv()
        far = jnp.where(behind, zin[h].astype(F32), 0.0)
        for j in range(4):
            pout[h, j] = (pre[h, j] + far).astype(BF16)
        ph2 += [send(pout.at[h, j], pfx.at[rows(x * 2 + h, BLK)], at_x(j)) for j in xs]
        pfx[rows(x * 2 + h, BLK)] = pout[h, x]
    out.append(dq_out(3))
    fw = [dq_forward(0)]

    for c in ph2:
        c.wait_recv()
    mine = pfx[...].astype(F32) + att[core].astype(F32)
    tot2 = xin
    tot2[...] = (mine + xin[...].astype(F32)).astype(BF16)
    back = send(tot2, hid.at[core], other_core)
    hid[core] = mine.astype(BF16)

    ld_down.wait()
    lt = []
    for m in (core, 1 - core):
        if lt:
            back.wait_recv()
        latp[m] = jnp.dot(hid[m], wd[...], preferred_element_type=F32).astype(BF16)
        lt.append([
            send(latp.at[m, rows(j, SUB)], latr.at[k, m], at_tensor(j)) for k, j in enumerate(tens)
        ])
    fw.append(dq_forward(1))

    for m in range(2):
        for q in range(4):
            for e in range(0, DSH, 64):
                at = q * DSH + e
                base = at // 128 * 128
                if at % 128 == 0 and e + 128 <= DSH:
                    htl[q, e:e + 128, m * TOK:(m + 1) * TOK] = hid[m, :, at:at + 128].T
                elif at % 128 == 0:
                    htl[q, e:e + 64, m * TOK:(m + 1) * TOK] = hid[m, :, base:base + 128].T[0:64]
                elif e == 0:
                    htl[q, 0:64, m * TOK:(m + 1) * TOK] = hid[m, :, base:base + 128].T[64:128]
    hall[d] = htl[d]

    def total(part, recv, m):
        v = part[m, rows(t, SUB)].astype(F32)
        for k in range(3):
            v = v + recv[k, m].astype(F32)
        return v

    g = gain[...].astype(F32)
    an = []
    for n, m in enumerate((core, 1 - core)):
        for c in lt[n]:
            c.wait_recv()
        lat = total(latp, latr, m)
        inv = lax.rsqrt(jnp.mean(lat * lat, axis=-1, keepdims=True) + EPSILON)
        nz[t, m] = (lat * inv * g).astype(BF16)
        an.append([send(nz.at[t, m], nz.at[t, m], at_tensor(j)) for j in tens])

    def hi_lo(v):
        high = v.astype(BF16).astype(F32)
        return jnp.concatenate([high, v - high, jnp.zeros((4, 128), F32)], axis=0).astype(BF16)

    def gain_rows(parts):
        v = jnp.zeros((16, 128), F32)
        for p in parts:
            v = v + p.astype(F32)
        return v[0:6] + v[6:12]

    for c in gn:
        c.wait_recv()
    part = jnp.zeros((1, QL), F32)
    for m in range(2):
        lat = total(latp, latr, m)
        inv = lax.rsqrt(jnp.mean(lat * lat, axis=-1, keepdims=True) + EPSILON)
        gnrm = total(gnp, gnr, m)
        scaled = gnrm * g
        back_mean = jnp.mean(scaled * lat, axis=-1, keepdims=True)
        gz[t, m * SUB:(m + 1) * SUB] = (
            inv * scaled - lat * (inv * inv * inv) * back_mean
        ).astype(BF16)
        part = part + jnp.sum(gnrm * lat * inv, axis=0, keepdims=True)
    gp[t] = hi_lo(
        jnp.concatenate([part[:, q * 128:(q + 1) * 128] for q in range(QL // 128)], axis=0)
    )

    for n, m in enumerate((core, 1 - core)):
        for c in an[n]:
            c.wait_recv()
        if n == 1:
            ag = [send(gz.at[t], gz.at[t], at_tensor(j)) for j in tens]
            gq = [send(gp.at[t], gp.at[t], at_tensor(j)) for j in tens]
        full = jnp.concatenate([nz[k, m] for k in range(4)], axis=0)
        lanes = pl.ds(pl.multiple_of(m * TOK, TOK), TOK)
        for q in range(QL // 64):
            if q % 2 == 0:
                tr = full[:, q * 64:q * 64 + 128].T
            dst, off = q * 64 // USH, q * 64 % USH
            ntl[dst, off:off + 64, lanes] = tr[(q % 2) * 64:(q % 2) * 64 + 64]
    nt = [send(ntl.at[j], nall.at[d], at_dp(j)) for j in dps]
    nall[d] = ntl[d]

    for c in nt:
        c.wait_recv()
    ups = []

    def grad_up(n):
        for c in (out[n][2], out[n][3]) + fw[n]:
            c.wait_recv()
        acc = jnp.zeros((USH, UW), F32)
        for k in range(4):
            acc = acc + jnp.dot(
                nall[k], dq[k, :, n * UW:(n + 1) * UW], preferred_element_type=F32
            )
        ubuf[n] = acc.astype(BF16)
        ups.append(send(ubuf.at[n], u_rec.at[n], mirror))
        load(ubuf.at[n], u_own.at[n])

    fw.append(dq_forward(2))
    grad_up(0)
    fw.append(dq_forward(3))
    grad_up(1)

    for c in ag:
        c.wait_recv()
    for m in range(2):
        for k in range(4):
            gl[d, m * TOK + k * SUB:m * TOK + (k + 1) * SUB] = gz[k, m * SUB:(m + 1) * SUB]

    for c in gq:
        c.wait_recv()
    gg[d] = hi_lo(gain_rows([gp[k] for k in range(4)]))
    ga = []

    def cols(n):
        return pl.ds(*DCOLS[n])

    def gl_out(n):
        ga.append([
            send(gl.at[d, r, cols(n)], gl.at[d, r, cols(n)], at_dp(j))
            for r, j in ((lo, up), (hi, dn), (hi, up), (lo, dn))
        ])

    gl_out(0)
    gl_out(1)
    gs = [send(gg.at[d], gg.at[d], at_dp(j)) for j in dps]
    ht = [send(htl.at[j], hall.at[d], at_dp(j)) for j in dps]
    grad_up(2)
    grad_up(3)

    def gl_forward(n):
        ga[n][0].wait_recv()
        ga[n].append(send(gl.at[dn, lo, cols(n)], gl.at[dn, lo, cols(n)], at_dp(up)))
        ga[n][1].wait_recv()
        ga[n].append(send(gl.at[up, hi, cols(n)], gl.at[up, hi, cols(n)], at_dp(dn)))

    gl_forward(0)
    gl_out(2)
    gl_forward(1)

    for c in gs:
        c.wait_recv()
    sums = gain_rows([gg[k] for k in range(4)])
    sums = jnp.concatenate([sums[q:q + 1] for q in range(QL // 128)], axis=1)
    pick = sums[:, 0:USH]
    for q in range(1, 4):
        pick = jnp.where(d == q, sums[:, q * USH:(q + 1) * USH], pick)
    gbuf[...] = jnp.broadcast_to(pick, (16, USH)).astype(BF16)
    last = [send(gbuf, g_rec, mirror)]
    load(gbuf, g_own)

    for c in ht:
        c.wait_recv()
    for n in range(len(DCOLS)):
        if n == 1:
            gl_forward(2)
        for c in ga[n][2:]:
            c.wait_recv()
        acc = jnp.zeros((DSH, DCOLS[n][1]), F32)
        for k in range(4):
            acc = acc + jnp.dot(hall[k], gl[k, :, cols(n)], preferred_element_type=F32)
        dbuf[:, cols(n)] = acc.astype(BF16)
        last.append(send(dbuf.at[:, cols(n)], d_rec.at[:, cols(n)], mirror))
        load(dbuf.at[:, cols(n)], d_own.at[:, cols(n)])

    for c in ups + last:
        c.wait_recv()
    for c in loads[6:]:
        c.wait()
    for c in sent:
        c.wait_send()


def finish(u_own, u_rec, d_own, d_rec, g_own, g_rec, down, gain, up):
    for n in range(UCH // STEPS):
        both = u_own[n].astype(F32) + u_rec[n].astype(F32)
        up[:, n * UW:(n + 1) * UW] = both.astype(BF16)
    down[...] = (d_own[...].astype(F32) + d_rec[...].astype(F32)).astype(BF16)
    gain[...] = (g_own[0:1].astype(F32) + g_rec[0:1].astype(F32)).astype(BF16)


def local(attn_a, attn_b, w_down, q_gain, w_up, dq_a, dq_b):
    anywhere = pl.BlockSpec(memory_space=pl.ANY)
    vmem = pl.BlockSpec(memory_space=pltpu.VMEM)
    shapes = [
        (2, TOK, DM), (TOK, DM), (TOK, DM), (2, 4, BLK, DM), (2, 4, BLK, DM), (2, BLK, DM),
        (2, BLK, DM), (2, 4, BLK, DM), (TOK, DM), (2, TOK, DM),
        (4, 2 * TOK, HQ), (DM, QL), (QL, HQ),
        (2, TOK, QL), (3, 2, SUB, QL), (2, TOK, QL), (3, 2, SUB, QL),
        (4, 2, SUB, QL), (4, 2 * SUB, QL), (4, 16, 128),
        (4, USH, 2 * TOK), (4, USH, 2 * TOK), (4, 2 * TOK, QL), (4, 16, 128),
        (4, DSH, 2 * TOK), (4, DSH, 2 * TOK),
        (UCH, USH, UW), (DSH, QL), (16, USH),
    ]
    halves = [(UCH, USH, UW)] * 2 + [(DSH, QL)] * 2 + [(16, USH)] * 2
    parts = pl.pallas_call(
        kernel,
        out_shape=[jax.ShapeDtypeStruct(x, BF16) for x in halves],
        in_specs=[anywhere, anywhere, anywhere, vmem, anywhere, anywhere, anywhere],
        out_specs=[anywhere] * 6,
        scratch_shapes=[pltpu.VMEM(x, F32 if i == 4 else BF16) for i, x in enumerate(shapes)] + [
            pltpu.SemaphoreType.DMA((16,)),
            pltpu.SemaphoreType.DMA((NCOPY,)),
            pltpu.SemaphoreType.DMA((NCOPY,)),
        ],
        compiler_params=pltpu.CompilerParams(
            collective_id=0, has_side_effects=True, vmem_limit_bytes=56 * 2**20
        ),
        name="sections",
    )(attn_a[0], attn_b[0], w_down[0], q_gain, w_up[0], dq_a[0], dq_b[0])
    ublock = pl.BlockSpec((UCH // STEPS, USH, UW), lambda n: (n, 0, 0))
    dblock = pl.BlockSpec((DSH // STEPS, QL), lambda n: (n, 0))
    gblock = pl.BlockSpec((16, USH), lambda n: (0, 0))
    down, gain, up = pl.pallas_call(
        finish,
        grid=(STEPS,),
        out_shape=(
            jax.ShapeDtypeStruct((DSH, QL), BF16),
            jax.ShapeDtypeStruct((1, USH), BF16),
            jax.ShapeDtypeStruct((USH, HQ), BF16),
        ),
        in_specs=[ublock, ublock, dblock, dblock, gblock, gblock],
        out_specs=(
            dblock,
            pl.BlockSpec((1, USH), lambda n: (0, 0)),
            pl.BlockSpec((USH, HQ // STEPS), lambda n: (0, n)),
        ),
        compiler_params=pltpu.CompilerParams(vmem_limit_bytes=56 * 2**20),
        name="finish",
    )(*parts)
    return down[None], gain, up[None]


def solution(mesh):
    return jax.shard_map(
        local,
        mesh=mesh,
        in_specs=(
            P("section", "dp", "tensor"),
            P("section", "dp", "tensor"),
            P("section", "tensor", None),
            P("section", None),
            P("section", None, "tensor"),
            P("section", "dp", "tensor"),
            P("section", "dp", "tensor"),
        ),
        out_specs=(
            P("section", ("tensor", "dp"), None),
            P("section", "dp"),
            P("section", "dp", "tensor"),
        ),
        check_vma=False,
    )
```

```python
import functools

import jax
import jax.numpy as jnp
from jax import lax
from jax.experimental import pallas as pl
from jax.experimental.pallas import tpu as pltpu
from jax.sharding import PartitionSpec as P

EPSILON = 1e-06
MESH = pl.DeviceIdType.MESH
F32 = jnp.float32
BF16 = jnp.bfloat16

TOK = 128
DM = 1792
QL = 768
HQ = 3072
BLK = 16
SUB = TOK // 4
DSH = DM // 4
USH = QL // 4
UCH = 4
UW = HQ // UCH
DCOLS = ((0, 384), (384, 256), (640, 128))
NCOPY = 128
STEPS = 2


def rows(i, n):
    return pl.ds(pl.multiple_of(i * n, n), n)


def kernel(
    attn_a, attn_b, w_down, gain, w_up, dq_a, dq_b,
    u_sum, d_own, d_rec, g_own, g_rec,
    att, xin, tot, got, pre, zout, zin, pout, pfx, hid, dq, wd, wu,
    gnp, gnr, latp, latr, nz, gz, gp, ntl, nall, gl, gg, htl, hall,
    ubuf, urec, usum, dbuf, gbuf,
    lsem, ss, rs,
):
    s, t, d = lax.axis_index("section"), lax.axis_index("tensor"), lax.axis_index("dp")
    chip, core = s // 2, s % 2

    zlo, x = chip // 4, chip % 4

    def at_x(j):
        return (zlo * 8 + j * 2 + core, t, d)

    def at_tensor(j):
        return (s, j, d)

    def at_dp(j):
        return (s, t, j)

    other_core = (chip * 2 + 1 - core, t, d)
    mirror = (15 - s, t, d)
    other_row = ((s + 8) % 16, t, d)
    xs = [((x + k) % 4) for k in range(1, 4)]
    tens = [((t + k) % 4) for k in range(1, 4)]
    dps = [((d + k) % 4) for k in range(1, 4)]
    up, dn = (d + 1) % 4, (d + 3) % 4
    lo, hi = pl.ds(0, TOK), pl.ds(TOK, TOK)

    counter = [0]
    sent = []

    def send(src, dst, to):
        i = counter[0]
        counter[0] += 1
        assert i < NCOPY
        copy = pltpu.make_async_remote_copy(
            src_ref=src, dst_ref=dst, send_sem=ss.at[i], recv_sem=rs.at[i],
            device_id=to, device_id_type=MESH,
        )
        copy.start()
        sent.append(copy)
        return copy

    loads = []

    def load(src, dst):
        c = pltpu.make_async_copy(src, dst, lsem.at[len(loads)])
        c.start()
        loads.append(c)
        return c

    ld_a = load(attn_a, att.at[0])
    ld_b = load(attn_b, att.at[1])

    barrier = pltpu.get_barrier_semaphore()
    partners = (
        [other_core, mirror, other_row]
        + [at_x(j) for j in xs]
        + [at_tensor(j) for j in tens]
        + [at_dp(j) for j in dps]
    )
    for p in partners:
        pl.semaphore_signal(barrier, inc=1, device_id=p, device_id_type=MESH)
    pl.semaphore_wait(barrier, len(partners))

    def dq_out(h):
        c = pl.ds(h * UW, UW)
        return (
            send(dq_a.at[:, c], dq.at[d, lo, c], at_dp(up)),
            send(dq_b.at[:, c], dq.at[d, hi, c], at_dp(dn)),
            send(dq_b.at[:, c], dq.at[d, hi, c], at_dp(up)),
            send(dq_a.at[:, c], dq.at[d, lo, c], at_dp(dn)),
        )

    def dq_forward(h):
        c = pl.ds(h * UW, UW)
        out[h][0].wait_recv()
        f = send(dq.at[dn, lo, c], dq.at[dn, lo, c], at_dp(up))
        out[h][1].wait_recv()
        return f, send(dq.at[up, hi, c], dq.at[up, hi, c], at_dp(dn))

    ld_a.wait()
    ld_b.wait()
    swap = send(att.at[1 - core], xin, other_core)
    out = [dq_out(0), dq_out(1)]
    ld_qa = load(dq_a, dq.at[d, lo])
    ld_qb = load(dq_b, dq.at[d, hi])
    ld_up = load(w_up, wu)
    ld_down = load(w_down, wd)

    swap.wait_recv()
    tot[...] = (att[core].astype(F32) + xin[...].astype(F32)).astype(BF16)
    ph1 = []
    for h in range(2):
        ph1.append([send(tot.at[rows(j * 2 + h, BLK)], got.at[h, x], at_x(j)) for j in xs])
        got[h, x] = tot[rows(x * 2 + h, BLK)]

    ld_qa.wait()
    ld_qb.wait()
    ld_up.wait()
    for m in range(2):
        gnp[m] = lax.dot_general(
            dq[d, m * TOK:(m + 1) * TOK], wu[...], (((1,), (1,)), ((), ())),
            preferred_element_type=F32,
        ).astype(BF16)

    totals = []
    for h in range(2):
        for c in ph1[h]:
            c.wait_recv()
        run = jnp.zeros((BLK, DM), F32)
        for i in range(4):
            j = i + core * (3 - 2 * i)
            pre[h, j] = run
            run = run + got[h, j].astype(F32)
        zout[h] = run.astype(BF16)
        totals.append(send(zout.at[h], zin.at[h], other_row))

    gn = [send(gnp.at[:, rows(j, SUB)], gnr.at[k], at_tensor(j)) for k, j in enumerate(tens)]
    out.append(dq_out(2))

    ph2 = []
    behind = zlo + core == 1
    for h in range(2):
        totals[h].wait_recv()
        far = jnp.where(behind, zin[h].astype(F32), 0.0)
        for j in range(4):
            pout[h, j] = (pre[h, j] + far).astype(BF16)
        ph2 += [send(pout.at[h, j], pfx.at[rows(x * 2 + h, BLK)], at_x(j)) for j in xs]
        pfx[rows(x * 2 + h, BLK)] = pout[h, x]
    out.append(dq_out(3))
    fw = [dq_forward(0)]

    for c in ph2:
        c.wait_recv()
    mine = pfx[...].astype(F32) + att[core].astype(F32)
    tot2 = xin
    tot2[...] = (mine + xin[...].astype(F32)).astype(BF16)
    back = send(tot2, hid.at[core], other_core)
    hid[core] = mine.astype(BF16)

    ld_down.wait()
    lt = []
    for m in (core, 1 - core):
        if lt:
            back.wait_recv()
        latp[m] = jnp.dot(hid[m], wd[...], preferred_element_type=F32).astype(BF16)
        lt.append([
            send(latp.at[m, rows(j, SUB)], latr.at[k, m], at_tensor(j)) for k, j in enumerate(tens)
        ])
    fw.append(dq_forward(1))

    for m in range(2):
        for q in range(4):
            for e in range(0, DSH, 64):
                at = q * DSH + e
                base = at // 128 * 128
                if at % 128 == 0 and e + 128 <= DSH:
                    htl[q, e:e + 128, m * TOK:(m + 1) * TOK] = hid[m, :, at:at + 128].T
                elif at % 128 == 0:
                    htl[q, e:e + 64, m * TOK:(m + 1) * TOK] = hid[m, :, base:base + 128].T[0:64]
                elif e == 0:
                    htl[q, 0:64, m * TOK:(m + 1) * TOK] = hid[m, :, base:base + 128].T[64:128]
    hall[d] = htl[d]

    def total(part, recv, m):
        v = part[m, rows(t, SUB)].astype(F32)
        for k in range(3):
            v = v + recv[k, m].astype(F32)
        return v

    g = gain[...].astype(F32)
    an = []
    for n, m in enumerate((core, 1 - core)):
        for c in lt[n]:
            c.wait_recv()
        lat = total(latp, latr, m)
        inv = lax.rsqrt(jnp.mean(lat * lat, axis=-1, keepdims=True) + EPSILON)
        nz[t, m] = (lat * inv * g).astype(BF16)
        an.append([send(nz.at[t, m], nz.at[t, m], at_tensor(j)) for j in tens])

    def hi_lo(v):
        high = v.astype(BF16).astype(F32)
        return jnp.concatenate([high, v - high, jnp.zeros((4, 128), F32)], axis=0).astype(BF16)

    def gain_rows(parts):
        v = jnp.zeros((16, 128), F32)
        for p in parts:
            v = v + p.astype(F32)
        return v[0:6] + v[6:12]

    for c in gn:
        c.wait_recv()
    part = jnp.zeros((1, QL), F32)
    for m in range(2):
        lat = total(latp, latr, m)
        inv = lax.rsqrt(jnp.mean(lat * lat, axis=-1, keepdims=True) + EPSILON)
        gnrm = total(gnp, gnr, m)
        scaled = gnrm * g
        back_mean = jnp.mean(scaled * lat, axis=-1, keepdims=True)
        gz[t, m * SUB:(m + 1) * SUB] = (
            inv * scaled - lat * (inv * inv * inv) * back_mean
        ).astype(BF16)
        part = part + jnp.sum(gnrm * lat * inv, axis=0, keepdims=True)
    gp[t] = hi_lo(
        jnp.concatenate([part[:, q * 128:(q + 1) * 128] for q in range(QL // 128)], axis=0)
    )

    for n, m in enumerate((core, 1 - core)):
        for c in an[n]:
            c.wait_recv()
        if n == 1:
            ag = [send(gz.at[t], gz.at[t], at_tensor(j)) for j in tens]
            gq = [send(gp.at[t], gp.at[t], at_tensor(j)) for j in tens]
        full = jnp.concatenate([nz[k, m] for k in range(4)], axis=0)
        lanes = pl.ds(pl.multiple_of(m * TOK, TOK), TOK)
        for q in range(QL // 64):
            if q % 2 == 0:
                tr = full[:, q * 64:q * 64 + 128].T
            dst, off = q * 64 // USH, q * 64 % USH
            ntl[dst, off:off + 64, lanes] = tr[(q % 2) * 64:(q % 2) * 64 + 64]
    nt = [send(ntl.at[j], nall.at[d], at_dp(j)) for j in dps]
    nall[d] = ntl[d]

    for c in nt:
        c.wait_recv()
    ups = []

    def grad_up(n):
        for c in (out[n][2], out[n][3]) + fw[n]:
            c.wait_recv()
        acc = jnp.zeros((USH, UW), F32)
        for k in range(4):
            acc = acc + jnp.dot(
                nall[k], dq[k, :, n * UW:(n + 1) * UW], preferred_element_type=F32
            )
        ubuf[n] = acc.astype(BF16)
        ups.append(send(ubuf.at[n], urec.at[n], mirror))

    fw.append(dq_forward(2))
    grad_up(0)
    fw.append(dq_forward(3))
    grad_up(1)

    for c in ag:
        c.wait_recv()
    for m in range(2):
        for k in range(4):
            gl[d, m * TOK + k * SUB:m * TOK + (k + 1) * SUB] = gz[k, m * SUB:(m + 1) * SUB]

    for c in gq:
        c.wait_recv()
    gg[d] = hi_lo(gain_rows([gp[k] for k in range(4)]))
    ga = []

    def cols(n):
        return pl.ds(*DCOLS[n])

    def gl_out(n):
        ga.append([
            send(gl.at[d, r, cols(n)], gl.at[d, r, cols(n)], at_dp(j))
            for r, j in ((lo, up), (hi, dn), (hi, up), (lo, dn))
        ])

    gl_out(0)
    gl_out(1)
    gs = [send(gg.at[d], gg.at[d], at_dp(j)) for j in dps]
    ht = [send(htl.at[j], hall.at[d], at_dp(j)) for j in dps]
    grad_up(2)
    grad_up(3)

    def gl_forward(n):
        ga[n][0].wait_recv()
        ga[n].append(send(gl.at[dn, lo, cols(n)], gl.at[dn, lo, cols(n)], at_dp(up)))
        ga[n][1].wait_recv()
        ga[n].append(send(gl.at[up, hi, cols(n)], gl.at[up, hi, cols(n)], at_dp(dn)))

    gl_forward(0)
    gl_out(2)
    gl_forward(1)

    for c in gs:
        c.wait_recv()
    sums = gain_rows([gg[k] for k in range(4)])
    sums = jnp.concatenate([sums[q:q + 1] for q in range(QL // 128)], axis=1)
    pick = sums[:, 0:USH]
    for q in range(1, 4):
        pick = jnp.where(d == q, sums[:, q * USH:(q + 1) * USH], pick)
    gbuf[...] = jnp.broadcast_to(pick, (16, USH)).astype(BF16)
    last = [send(gbuf, g_rec, mirror)]
    load(gbuf, g_own)

    for c in ht:
        c.wait_recv()
    for n in range(len(DCOLS)):
        if n == 1:
            gl_forward(2)
        for c in ga[n][2:]:
            c.wait_recv()
        acc = jnp.zeros((DSH, DCOLS[n][1]), F32)
        for k in range(4):
            acc = acc + jnp.dot(hall[k], gl[k, :, cols(n)], preferred_element_type=F32)
        dbuf[:, cols(n)] = acc.astype(BF16)
        last.append(send(dbuf.at[:, cols(n)], d_rec.at[:, cols(n)], mirror))
        load(dbuf.at[:, cols(n)], d_own.at[:, cols(n)])

    for n in range(UCH):
        ups[n].wait_recv()
        usum[n] = (ubuf[n].astype(F32) + urec[n].astype(F32)).astype(BF16)
        load(usum.at[n], u_sum.at[n])
    for c in last:
        c.wait_recv()
    for c in loads[6:]:
        c.wait()
    for c in sent:
        c.wait_send()


def finish(u_sum, d_own, d_rec, g_own, g_rec, down, gain, up):
    for n in range(UCH // STEPS):
        up[:, n * UW:(n + 1) * UW] = u_sum[n]
    down[...] = (d_own[...].astype(F32) + d_rec[...].astype(F32)).astype(BF16)
    gain[...] = (g_own[0:1].astype(F32) + g_rec[0:1].astype(F32)).astype(BF16)


def local(attn_a, attn_b, w_down, q_gain, w_up, dq_a, dq_b):
    anywhere = pl.BlockSpec(memory_space=pl.ANY)
    vmem = pl.BlockSpec(memory_space=pltpu.VMEM)
    shapes = [
        (2, TOK, DM), (TOK, DM), (TOK, DM), (2, 4, BLK, DM), (2, 4, BLK, DM), (2, BLK, DM),
        (2, BLK, DM), (2, 4, BLK, DM), (TOK, DM), (2, TOK, DM),
        (4, 2 * TOK, HQ), (DM, QL), (QL, HQ),
        (2, TOK, QL), (3, 2, SUB, QL), (2, TOK, QL), (3, 2, SUB, QL),
        (4, 2, SUB, QL), (4, 2 * SUB, QL), (4, 16, 128),
        (4, USH, 2 * TOK), (4, USH, 2 * TOK), (4, 2 * TOK, QL), (4, 16, 128),
        (4, DSH, 2 * TOK), (4, DSH, 2 * TOK),
        (UCH, USH, UW), (UCH, USH, UW), (UCH, USH, UW), (DSH, QL), (16, USH),
    ]
    halves = [(UCH, USH, UW)] + [(DSH, QL)] * 2 + [(16, USH)] * 2
    parts = pl.pallas_call(
        kernel,
        out_shape=[jax.ShapeDtypeStruct(x, BF16) for x in halves],
        in_specs=[anywhere, anywhere, anywhere, vmem, anywhere, anywhere, anywhere],
        out_specs=[anywhere] * 5,
        scratch_shapes=[pltpu.VMEM(x, F32 if i == 4 else BF16) for i, x in enumerate(shapes)] + [
            pltpu.SemaphoreType.DMA((16,)),
            pltpu.SemaphoreType.DMA((NCOPY,)),
            pltpu.SemaphoreType.DMA((NCOPY,)),
        ],
        compiler_params=pltpu.CompilerParams(
            collective_id=0, has_side_effects=True, vmem_limit_bytes=56 * 2**20
        ),
        name="sections",
    )(attn_a[0], attn_b[0], w_down[0], q_gain, w_up[0], dq_a[0], dq_b[0])
    ublock = pl.BlockSpec((UCH // STEPS, USH, UW), lambda n: (n, 0, 0))
    dblock = pl.BlockSpec((DSH // STEPS, QL), lambda n: (n, 0))
    gblock = pl.BlockSpec((16, USH), lambda n: (0, 0))
    down, gain, up = pl.pallas_call(
        finish,
        grid=(STEPS,),
        out_shape=(
            jax.ShapeDtypeStruct((DSH, QL), BF16),
            jax.ShapeDtypeStruct((1, USH), BF16),
            jax.ShapeDtypeStruct((USH, HQ), BF16),
        ),
        in_specs=[ublock, dblock, dblock, gblock, gblock],
        out_specs=(
            dblock,
            pl.BlockSpec((1, USH), lambda n: (0, 0)),
            pl.BlockSpec((USH, HQ // STEPS), lambda n: (0, n)),
        ),
        compiler_params=pltpu.CompilerParams(vmem_limit_bytes=56 * 2**20),
        name="finish",
    )(*parts)
    return down[None], gain, up[None]


def solution(mesh):
    return jax.shard_map(
        local,
        mesh=mesh,
        in_specs=(
            P("section", "dp", "tensor"),
            P("section", "dp", "tensor"),
            P("section", "tensor", None),
            P("section", None),
            P("section", None, "tensor"),
            P("section", "dp", "tensor"),
            P("section", "dp", "tensor"),
        ),
        out_specs=(
            P("section", ("tensor", "dp"), None),
            P("section", "dp"),
            P("section", "dp", "tensor"),
        ),
        check_vma=False,
    )
```
